128 devices in a mesh: req: 16 (over y, x), tp: 8 (over z, core).
Axes of the slice: x: 4, y: 4, z: 4, core: 2. Of those that a mesh axis runs over, the one named last changes fastest.
Arguments:
- tokens: bfloat16 [16, 384, 8192], P('req', 'tp'), may hold values from -6 to 6
- norm_gain: bfloat16 [8192], replicated, may hold values from 0.099609375 to 1.8984375
- w_query: bfloat16 [8192, 8192], P(None, 'tp'), may hold values from -3 to 3
- w_key: bfloat16 [8192, 1024], P(None, 'tp'), may hold values from -1 to 1
- w_value: bfloat16 [8192, 1024], P(None, 'tp'), may hold values from -0.0625 to 0.0625
- store_keys: bfloat16 [64, 512, 8, 128], P('req', None, 'tp'), may hold values from -6 to 6
- store_values: bfloat16 [64, 512, 8, 128], P('req', None, 'tp'), may hold values from -6 to 6
- block_slot: int32 [64], replicated, may hold values from 0 to 63, as said below
- retrieval: int32 [16, 8], replicated, may hold values from 0 to 63, as said below
- sel_index: int32 [16, 384], P('req'), may hold values from 0 to 4095, as said below
Outputs:
- attended: bfloat16 [16, 384, 8192], P('req', None, 'tp')
The draws below stay inside these ranges and needn't reach their ends.
Inputs may be any that keep to these rules, and one draw needn't show every extreme that they name: `block_slot`: a permutation: slots 4 * s to 4 * s + 3 lie on store device s. `retrieval`: a request's 8 blocks lie on 8 different store devices. `sel_index`: a request's positions rise strictly, the first is 0 and the last 4095.
All inputs are finite; a program needn't handle non-finite values.
Results may differ from the reference program's by a relative error of at most 0.0064.
Values may be sent and summed in bfloat16 or wider, within the bound.
No kernel may reach another device: no remote copies, remote signals or barrier semaphores. Data moves between devices by JAX's collectives and lax.ppermute only.
A program may use at most 192 MiB of HBM per device.

```python
import jax
import jax.numpy as jnp
from jax import lax

D = 8192
HEADS = 64
KVH = 8
HD = 128
BLOCK = 512
TOPK = 8
SEL = 384
STORE_DEV = 4
CTX = 4096
REQS = 16
BLOCKS = 64


def catalog(key):
    return jax.random.permutation(key, BLOCKS).astype(jnp.int32)


def key_matrix(key):
    shared_key = jax.random.fold_in(key, 11)
    fresh = jax.random.normal(shared_key, (D, KVH * HD), jnp.float32)
    return jnp.clip(fresh, -5.0, 5.0) * float(D) ** (-0.5)


def draw_block_slot(key, part):
    placed = catalog(key)
    return placed


def draw_retrieval(key, part):
    placed = catalog(key)
    key = jax.random.fold_in(key, 2)
    holder = jnp.argsort(placed).astype(jnp.int32)
    devices = BLOCKS // STORE_DEV
    key_hot, key_jit, key_loc = jax.random.split(key, 3)
    hotness = jax.random.randint(key_hot, (devices,), 0, 4)
    jitter = jax.random.randint(key_jit, (REQS, devices), 0, 1024)
    ranking = (jitter + 512 * hotness[None, :]) * devices + jnp.arange(devices)[None, :]
    ignored, stores = lax.top_k(ranking, TOPK)
    local_slot = jax.random.randint(key_loc, (REQS, TOPK), 0, STORE_DEV)
    return holder[stores * STORE_DEV + local_slot].astype(jnp.int32)


def draw_sel_index(key, part):
    key = jax.random.fold_in(key, 3)
    ranking = jax.random.randint(key, (REQS, CTX - 2), 0, 262144) * CTX + jnp.arange(CTX - 2)[None, :]
    ignored, chosen = lax.top_k(ranking, SEL - 2)
    interior = jnp.sort(chosen + 1, axis=1)
    first = jnp.zeros((REQS, 1), jnp.int32)
    final = jnp.full((REQS, 1), CTX - 1, jnp.int32)
    return jnp.concatenate([first, interior.astype(jnp.int32), final], axis=1)


def draw_tokens(key, part):
    key = jax.random.fold_in(key, 4)
    key_rows = jax.random.fold_in(key, 0)
    fresh = jax.random.normal(key_rows, (REQS, SEL, D), jnp.float32)
    return jnp.clip(fresh, -6.0, 6.0).astype(jnp.bfloat16)


def draw_w_key(key, part):
    shared = key_matrix(key)
    return shared.astype(jnp.bfloat16)


def draw_w_query(key, part):
    key = jax.random.fold_in(key, 5)
    key_fresh = jax.random.fold_in(key, 0)
    fresh = jnp.clip(jax.random.normal(key_fresh, (D, HEADS * HD), jnp.float32), -5.0, 5.0) * float(D) ** (-0.5)
    return fresh.astype(jnp.bfloat16)


def steps_of(stream_key, extent, pieces, low, high):
    gain = 1.0
    for position, shards_of in pieces:
        heights = jax.random.uniform(jax.random.fold_in(jax.random.fold_in(stream_key, 6), position), (shards_of,), jnp.float32, low / len(pieces), high / len(pieces))
        gain = gain * jnp.repeat(jnp.exp(heights), extent[position] // shards_of).reshape((-1,) + (1,) * (len(extent) - 1 - position))
    return gain


def centred(own_key, shape, deviation, most, cuts=(), held_as=jnp.bfloat16):
    values = deviation * jax.random.normal(own_key, shape, jnp.float32)
    if cuts:
        values = values * steps_of(own_key, shape, cuts, -0.22, 0.18)
    return jnp.clip(values, -most, most).astype(held_as)


def setup_inputs(seed: int = 0) -> dict:
    arg_keys = jax.random.split(jax.random.key(seed), 11)
    return {
        "tokens": draw_tokens(jax.random.fold_in(arg_keys[10], 71), 0),
        "norm_gain": jnp.clip(1.0 + 0.18 * jax.random.normal(arg_keys[1], (D,), jnp.float32), 0.099609375, 1.8984375).astype(jnp.bfloat16),
        "w_query": draw_w_query(jax.random.fold_in(arg_keys[10], 71), 0),
        "w_key": draw_w_key(jax.random.fold_in(arg_keys[10], 71), 0),
        "w_value": centred(arg_keys[4], (D, KVH * HD), D ** -0.5, 0.0625, ((1, 8),)),
        "store_keys": centred(arg_keys[5], (BLOCKS, BLOCK, KVH, HD), 1.0, 6.0, ((0, 16), (2, 8))),
        "store_values": centred(arg_keys[6], (BLOCKS, BLOCK, KVH, HD), 1.0, 6.0, ((0, 16), (2, 8))),
        "block_slot": draw_block_slot(jax.random.fold_in(arg_keys[10], 71), 0),
        "retrieval": draw_retrieval(jax.random.fold_in(arg_keys[10], 71), 0),
        "sel_index": draw_sel_index(jax.random.fold_in(arg_keys[10], 71), 0),
    }


def rotate(values, positions):
    half_dim = values.shape[-1] // 2
    frequency = 500000.0 ** (-(2.0 / values.shape[-1]) * jnp.arange(half_dim).astype(jnp.float32))
    angles = positions.astype(jnp.float32)[:, None] * frequency[None, :]
    cosine = jnp.cos(angles)[:, None, :]
    sines = jnp.sin(angles)[:, None, :]
    first = values[..., :half_dim]
    second = values[..., half_dim:]
    return jnp.concatenate([first * cosine - second * sines, second * cosine + first * sines], axis=-1)

def reference(tokens, norm_gain, w_query, w_key, w_value, store_keys, store_values, block_slot, retrieval, sel_index):
    group = HEADS // KVH

    def one_request(request):
        hidden = tokens[request].astype(jnp.float32)
        scale_rows = lax.rsqrt(lax.optimization_barrier(jnp.mean(hidden * hidden, axis=-1, keepdims=True)) + 1e-05)
        normed = (hidden * scale_rows * norm_gain.astype(jnp.float32)).astype(jnp.bfloat16)
        query_raw = jnp.dot(normed, w_query, preferred_element_type=jnp.float32).reshape(SEL, HEADS, HD)
        new_keys = jnp.dot(normed, w_key, preferred_element_type=jnp.float32).astype(jnp.bfloat16).reshape(SEL, KVH, HD)
        new_values = jnp.dot(normed, w_value, preferred_element_type=jnp.float32).astype(jnp.bfloat16).reshape(SEL, KVH, HD)
        positions = sel_index[request]
        queries = rotate(query_raw, positions).astype(jnp.bfloat16)
        chosen = block_slot[retrieval[request]]
        ctx_keys = store_keys[chosen].reshape(CTX, KVH, HD).at[positions].set(new_keys)
        ctx_values = store_values[chosen].reshape(CTX, KVH, HD).at[positions].set(new_values)
        everywhere = jnp.arange(CTX).astype(jnp.int32)
        rot_keys = rotate(ctx_keys.astype(jnp.float32), everywhere).astype(jnp.bfloat16)
        grouped = queries.reshape(SEL, KVH, group, HD).astype(jnp.float32)
        scores = jnp.einsum('sngd,cnd->ngsc', grouped, rot_keys.astype(jnp.float32)) / jnp.sqrt(jnp.float32(HD))
        visible = everywhere[None, :] <= positions[:, None]
        scores = jnp.where(visible[None, None], scores, -jnp.inf)
        highest = lax.optimization_barrier(jnp.max(scores, axis=-1, keepdims=True))
        expos = jnp.exp(scores - highest)
        weights = (expos / lax.optimization_barrier(jnp.sum(expos, axis=-1, keepdims=True))).astype(jnp.bfloat16)
        mixed = jnp.einsum('ngsc,cnd->sngd', weights.astype(jnp.float32), ctx_values.astype(jnp.float32))
        return mixed.reshape(SEL, HEADS * HD).astype(jnp.bfloat16)
    return lax.map(one_request, jnp.arange(REQS).astype(jnp.int32))
```

```python
import functools

import jax
import jax.numpy as jnp
from jax import lax
from jax.experimental import pallas as pl
from jax.experimental.pallas import tpu as pltpu
from jax.sharding import PartitionSpec as P

BF16 = jnp.bfloat16
F32 = jnp.float32
SIDE = 4
ROWS = 64
THETA = 500000.0
EPS = 1e-05
HIDDEN_POS = 1 << 30
MIB = 1 << 20


def move(value, step):
    pairs = []
    for y in range(SIDE):
        for x in range(SIDE):
            for z in range(SIDE):
                for core in range(2):
                    ty, tx, tz, tc = step(y, x, z, core)
                    source = ((y * SIDE + x) * SIDE + z) * 2 + core
                    target = (((ty % SIDE) * SIDE + tx % SIDE) * SIDE + tz % SIDE) * 2 + tc
                    pairs.append((source, target))
    return lax.ppermute(value, ("req", "tp"), pairs)


def way(core):
    return 1 if core == 0 else -1


def along_x(value, sign):
    return move(value, lambda y, x, z, c: (y, x + sign * way(c), z, c))


def along_y(value, sign):
    return move(value, lambda y, x, z, c: (y + sign * way(c), x, z, c))


def along_z(value):
    return move(value, lambda y, x, z, c: (y, x, z + way(c), c))


def other_core(value):
    return move(value, lambda y, x, z, c: (y, x, z, 1 - c))


def norm_kernel(tokens_ref, gain_ref, out_ref):
    hidden = tokens_ref[...].astype(F32)
    scale = lax.rsqrt(jnp.mean(hidden * hidden, axis=-1, keepdims=True) + EPS)
    out_ref[...] = (hidden * scale * gain_ref[...].astype(F32)).astype(BF16)


def normalise(tokens, gain):
    return pl.pallas_call(
        norm_kernel,
        out_shape=jax.ShapeDtypeStruct(tokens.shape, BF16),
        compiler_params=pltpu.CompilerParams(vmem_limit_bytes=24 * MIB),
        name="norm",
    )(tokens, gain.reshape(1, -1))


def pick_kernel(index_ref, *refs):
    sources, (k_fwd, k_back, v_fwd, v_back), sems = refs[:8], refs[8:12], refs[12]
    copies = []
    for tensor, (fwd, back) in enumerate(((k_fwd, k_back), (v_fwd, v_back))):
        for target in range(3):
            for slot in range(4):
                dest = fwd.at[target * 4 + slot] if target < 2 else back.at[slot]
                n = tensor * 12 + target * 4 + slot
                copies.append(
                    pltpu.make_async_copy(
                        sources[tensor * 4 + slot].at[index_ref[n]], dest, sems.at[n]
                    )
                )
    for copy in copies:
        copy.start()
    for copy in copies:
        copy.wait()


def pick(index, keys, values):
    _, tokens, dim = keys[0].shape
    any_spec = pl.BlockSpec(memory_space=pl.ANY)
    shapes = [jax.ShapeDtypeStruct((n, tokens, dim), BF16) for n in (8, 4, 8, 4)]
    return pl.pallas_call(
        pick_kernel,
        out_shape=shapes,
        in_specs=[pl.BlockSpec(memory_space=pltpu.SMEM)] + [any_spec] * 8,
        out_specs=[any_spec] * 4,
        scratch_shapes=[pltpu.SemaphoreType.DMA((24,))],
        compiler_params=pltpu.CompilerParams(vmem_limit_bytes=2 * MIB),
        cost_estimate=pl.CostEstimate(flops=0, bytes_accessed=6 * MIB, transcendentals=0),
        name="pick",
    )(index, *keys, *values)


def rope(values, cosine, sine):
    return values * cosine + pltpu.roll(values, 64, 1) * sine


def project_kernel(
    place_ref, p0, p1, p2, p3, p4, p5, p6, p7, wq_ref, wk_hbm, wv_hbm, cos_ref, sin_ref,
    q_ref, nk_ref, nv_ref, x_buf, wk_buf, wv_buf, x_sems, w_sems,
):
    step = pl.program_id(0)
    pieces = (p0, p1, p2, p3, p4, p5, p6, p7)
    rows = p0.shape[0]

    def piece_copy(n):
        at = pl.multiple_of(place_ref[n] * rows, 16)
        return pltpu.make_async_copy(pieces[n], x_buf.at[pl.ds(at, rows)], x_sems.at[n])

    k_copy = pltpu.make_async_copy(wk_hbm, wk_buf, w_sems.at[0])
    v_copy = pltpu.make_async_copy(wv_hbm, wv_buf, w_sems.at[1])

    @pl.when(step == 0)
    def _():
        for n in range(8):
            piece_copy(n).start()
        k_copy.start()
        v_copy.start()
        for n in range(8):
            piece_copy(n).wait()

    cosine = cos_ref[...]
    sine = sin_ref[...]

    @pl.when(step < 4)
    def _():
        raw = jnp.dot(x_buf[...], wq_ref[...], preferred_element_type=F32)
        for h in range(2):
            q_ref[h] = rope(raw[:, h * 128 : (h + 1) * 128], cosine, sine).astype(BF16)

    @pl.when(step == 4)
    def _():
        k_copy.wait()
        v_copy.wait()
        new_k = jnp.dot(x_buf[...], wk_buf[...], preferred_element_type=F32).astype(BF16)
        nk_ref[...] = rope(new_k.astype(F32), cosine, sine).astype(BF16)
        nv_ref[...] = jnp.dot(x_buf[...], wv_buf[...], preferred_element_type=F32).astype(BF16)


def project(place, pieces, w_query, w_key, w_value, cosine, sine):
    rows, width = pieces[0].shape
    sel = 8 * rows
    any_spec = pl.BlockSpec(memory_space=pl.ANY)
    whole = pl.BlockSpec((sel, 128), lambda i: (0, 0))
    last = lambda i: jnp.minimum(i, 3)
    return pl.pallas_call(
        project_kernel,
        grid=(5,),
        out_shape=[
            jax.ShapeDtypeStruct((8, sel, 128), BF16),
            jax.ShapeDtypeStruct((sel, 128), BF16),
            jax.ShapeDtypeStruct((sel, 128), BF16),
        ],
        in_specs=[pl.BlockSpec(memory_space=pltpu.SMEM)]
        + [any_spec] * 8
        + [pl.BlockSpec((width, 256), lambda i: (0, last(i))), any_spec, any_spec, whole, whole],
        out_specs=[pl.BlockSpec((2, sel, 128), lambda i: (last(i), 0, 0)), whole, whole],
        scratch_shapes=[
            pltpu.VMEM((sel, width), BF16),
            pltpu.VMEM((width, 128), BF16),
            pltpu.VMEM((width, 128), BF16),
            pltpu.SemaphoreType.DMA((8,)),
            pltpu.SemaphoreType.DMA((2,)),
        ],
        compiler_params=pltpu.CompilerParams(vmem_limit_bytes=40 * MIB),
        cost_estimate=pl.CostEstimate(
            flops=2 * sel * width * 1280, bytes_accessed=30 * MIB, transcendentals=0
        ),
        name="project",
    )(place, *pieces, w_query, w_key, w_value, cosine, sine)


def attend_kernel(
    where_ref, count_ref, q_ref, nk_ref, nv_ref, qpos_ref, kpos_ref, npos_ref, cos_ref, sin_ref, *refs
):
    keys, values, out_ref = refs[:7], refs[7:14], refs[14]
    k_buf, v_buf, nv_buf, s_buf, m_buf, acc, sems = refs[15:]
    block = k_buf.shape[1]
    blocks = k_buf.shape[0]
    heads, sel, dim = q_ref.shape
    ctx = block * blocks
    tall = heads * ROWS
    factor = 1.4426950408889634 / (dim ** 0.5)

    def k_dest(j):
        return k_buf.at[j]

    def v_dest(j):
        return v_buf.at[pl.ds(j * block, block), pl.ds(0, dim)]

    for j in range(blocks):
        for n in range(7):

            @pl.when(where_ref[0, j] == n)
            def _():
                pltpu.make_async_copy(keys[n].at[where_ref[1, j]], k_dest(j), sems.at[0, j]).start()

            @pl.when(where_ref[2, j] == n)
            def _():
                pltpu.make_async_copy(values[n].at[where_ref[3, j]], v_dest(j), sems.at[1, j]).start()

    v_buf[:, dim:] = jnp.ones((ctx, dim), BF16)
    nv_buf[:, dim:] = jnp.ones((sel, dim), BF16)
    nv_buf[:, :dim] = nv_ref[...]

    for j in range(blocks):
        pltpu.make_async_copy(keys[0].at[0], k_dest(j), sems.at[0, j]).wait()
        at = pl.ds(j * block, block)
        k_buf[j] = rope(k_buf[j].astype(F32), cos_ref[at, :], sin_ref[at, :]).astype(BF16)
    for j in range(blocks):
        pltpu.make_async_copy(values[0].at[0], v_dest(j), sems.at[1, j]).wait()

    def masked_scores(queries, key_block, key_pos, query_pos):
        width = key_block.shape[0]
        scores = lax.dot_general(
            queries, key_block, (((1,), (1,)), ((), ())), preferred_element_type=F32
        )
        reps = width // 128
        seen = key_pos <= jnp.concatenate([query_pos] * reps, axis=1)
        scores = jnp.where(seen[None], scores.reshape(heads, ROWS, width), -jnp.inf)
        scores = scores.reshape(tall, width)
        most = scores[:, :128]
        for n in range(1, reps):
            most = jnp.maximum(most, scores[:, n * 128 : (n + 1) * 128])
        return scores, most

    def tile(i, carry):
        rows = pl.ds(pl.multiple_of(i * ROWS, ROWS), ROWS)
        queries = q_ref[:, rows, :].reshape(tall, dim)
        query_pos = qpos_ref[rows, :]
        scores, most = masked_scores(queries, nk_ref[...], npos_ref[...], query_pos)
        s_buf[:, ctx:] = scores
        m_buf[...] = most
        count = count_ref[i]

        def first(j, carry):
            scores, most = masked_scores(
                q_ref[:, rows, :].reshape(tall, dim), k_buf[j], kpos_ref[pl.ds(j, 1), :], qpos_ref[rows, :]
            )
            s_buf[:, pl.ds(pl.multiple_of(j * block, block), block)] = scores
            m_buf[...] = jnp.maximum(m_buf[...], most)
            return carry

        lax.fori_loop(0, count, first, 0)
        m_buf[...] = jnp.broadcast_to(jnp.max(m_buf[...], axis=1, keepdims=True), (tall, 128))

        def expos(scores):
            most = jnp.concatenate([m_buf[...]] * (scores.shape[1] // 128), axis=1)
            return jnp.exp2((scores - most) * factor).astype(BF16)

        acc[...] = jnp.dot(expos(s_buf[:, ctx:]), nv_buf[...], preferred_element_type=F32)

        def second(j, carry):
            at = pl.ds(pl.multiple_of(j * block, block), block)
            acc[...] += jnp.dot(expos(s_buf[:, at]), v_buf[at, :], preferred_element_type=F32)
            return carry

        lax.fori_loop(0, count, second, 0)
        result = (acc[:, :dim] / acc[:, dim:]).astype(BF16)
        for h in range(heads):
            out_ref[rows, h * dim : (h + 1) * dim] = result[h * ROWS : (h + 1) * ROWS]
        return carry

    lax.fori_loop(0, sel // ROWS, tile, 0)


def attend(where, count, queries, new_k, new_v, qpos, kpos, npos, cosine, sine, keys, values):
    heads, sel, dim = queries.shape
    _, block, _ = keys[0].shape
    blocks = kpos.shape[0]
    ctx = block * blocks
    smem = pl.BlockSpec(memory_space=pltpu.SMEM)
    vmem = pl.BlockSpec(memory_space=pltpu.VMEM)
    any_spec = pl.BlockSpec(memory_space=pl.ANY)
    tall = heads * ROWS
    return pl.pallas_call(
        attend_kernel,
        out_shape=jax.ShapeDtypeStruct((sel, heads * dim), BF16),
        in_specs=[smem] * 2 + [vmem] * 8 + [any_spec] * 14,
        out_specs=vmem,
        scratch_shapes=[
            pltpu.VMEM((blocks, block, dim), BF16),
            pltpu.VMEM((ctx, 2 * dim), BF16),
            pltpu.VMEM((sel, 2 * dim), BF16),
            pltpu.VMEM((tall, ctx + sel), F32),
            pltpu.VMEM((tall, 128), F32),
            pltpu.VMEM((tall, 2 * dim), F32),
            pltpu.SemaphoreType.DMA((2, blocks)),
        ],
        compiler_params=pltpu.CompilerParams(vmem_limit_bytes=40 * MIB),
        cost_estimate=pl.CostEstimate(
            flops=4 * heads * sel * ctx * dim, bytes_accessed=8 * MIB, transcendentals=heads * sel * ctx
        ),
        name="attend",
    )(where, count, queries, new_k, new_v, qpos, kpos, npos, cosine, sine, *keys, *values)


def tables(positions):
    frequency = THETA ** (-(2.0 / 128) * jnp.arange(64).astype(F32))
    angles = positions.astype(F32)[:, None] * frequency[None, :]
    cosine, sine = jnp.cos(angles), jnp.sin(angles)
    return jnp.concatenate([cosine, cosine], axis=1), jnp.concatenate([-sine, sine], axis=1)


def order_of(offset, sign):
    return jnp.where(
        offset == 0, 0, jnp.where(offset == 2, 3, jnp.where(offset == (-sign) % SIDE, 1, 2))
    )


def on_device(
    tokens, norm_gain, w_query, w_key, w_value, store_keys, store_values, block_slot, retrieval, sel_index
):
    held, block, _, dim = store_keys.shape
    requests, chosen_count = retrieval.shape
    stores = block_slot.shape[0] // held
    req, tp = lax.axis_index("req"), lax.axis_index("tp")
    y, x = req // SIDE, req % SIDE
    z, core = tp // 2, tp % 2
    sign = 1 - 2 * core

    own_k = store_keys.reshape(held, block, dim)
    own_v = store_values.reshape(held, block, dim)
    k_one, k_two = along_x(own_k, 1), along_x(own_k, -1)
    v_one, v_two = along_y(own_v, 1), along_y(own_v, -1)
    normed = normalise(tokens[0], norm_gain)
    z_one = along_z(normed)
    k_far, v_far = along_x(k_one, 1), along_y(v_one, 1)
    z_two = along_z(z_one)
    z_far = along_z(z_two)
    mine = [normed, z_one, z_two, z_far]
    theirs = [other_core(piece) for piece in mine]
    row_k = [own_k, k_one, k_two, k_far]
    column_v = [own_v, v_one, v_two, v_far]

    hot = retrieval[:, :, None] == jnp.arange(block_slot.shape[0])[None, None, :]
    slots = jnp.sum(jnp.where(hot, block_slot[None, None, :], 0), axis=2)
    at_store = (slots // held)[:, :, None] == jnp.arange(stores)[None, None, :]
    wanted = jnp.sum(jnp.where(at_store, (slots % held)[:, :, None], 0), axis=1).reshape(-1)
    arrivals = [0, -sign, sign, 2]
    targets = [sign, 2, -sign]

    def node(yy, xx):
        return ((yy + SIDE) % SIDE) * SIDE + (xx + SIDE) % SIDE

    picks = [node(y + t, x) * stores + node(y, x + a) for t in targets for a in arrivals]
    picks += [node(y, x + t) * stores + node(y + a, x) for t in targets for a in arrivals]
    pick_at = jnp.stack(picks)
    entries = pick_at[:, None] == jnp.arange(requests * stores)[None, :]
    index = jnp.sum(jnp.where(entries, wanted[None, :], 0), axis=1).astype(jnp.int32)

    k_fwd, k_back, v_fwd, v_back = pick(index, row_k, column_v)
    k_fwd, k_back = along_y(k_fwd, 1), along_y(k_back, -1)
    v_fwd, v_back = along_x(v_fwd, 1), along_x(v_back, -1)
    k_last, v_last = along_y(k_fwd[4:], 1), along_x(v_fwd[4:], 1)
    keys = row_k + [k_fwd, k_back, k_last]
    values = column_v + [v_fwd, v_back, v_last]

    own_slots = jnp.sum(jnp.where((jnp.arange(requests) == req)[:, None], slots, 0), axis=0)
    store, local = own_slots // held, own_slots % held
    order_y = order_of((store // SIDE - y) % SIDE, sign)
    order_x = order_of((store % SIDE - x) % SIDE, sign)
    where = jnp.stack(
        [
            jnp.where(order_y == 0, order_x, 3 + order_y),
            jnp.where(order_y == 0, local, order_x),
            jnp.where(order_x == 0, order_y, 3 + order_x),
            jnp.where(order_x == 0, local, order_y),
        ]
    ).astype(jnp.int32)

    positions = sel_index[0]
    sel = positions.shape[0]
    ctx = chosen_count * block
    everywhere = jnp.arange(ctx, dtype=jnp.int32)
    replaced = jnp.any(positions[:, None] == everywhere[None, :], axis=0)
    kpos = jnp.where(replaced, HIDDEN_POS, everywhere).reshape(chosen_count, block)
    qpos = jnp.broadcast_to(positions[:, None], (sel, 128))
    count = positions[ROWS - 1 :: ROWS] // block + 1
    q_cos, q_sin = tables(positions)
    k_cos, k_sin = tables(everywhere)

    place = jnp.stack(
        [((z + s * sign + SIDE) % SIDE) * 2 + core for s in (0, -1, 2, 1)]
        + [((z + s * sign + SIDE) % SIDE) * 2 + 1 - core for s in (0, 1, 2, -1)]
    ).astype(jnp.int32)
    queries, new_k, new_v = project(place, mine + theirs, w_query, w_key, w_value, q_cos, q_sin)
    mixed = attend(
        where, count, queries, new_k, new_v, qpos, kpos, positions[None], k_cos, k_sin, keys, values
    )
    return mixed[None]


def solution(mesh):
    placed = (
        P("req", "tp", None),
        P(),
        P(None, "tp"),
        P(None, "tp"),
        P(None, "tp"),
        P("req", None, "tp", None),
        P("req", None, "tp", None),
        P(),
        P(),
        P("req", None),
    )
    return jax.shard_map(
        on_device, mesh=mesh, in_specs=placed, out_specs=P("req", None, "tp"), check_vma=False
    )
```

```python
import functools

import jax
import jax.numpy as jnp
from jax import lax
from jax.experimental import pallas as pl
from jax.experimental.pallas import tpu as pltpu
from jax.sharding import PartitionSpec as P

BF16 = jnp.bfloat16
F32 = jnp.float32
SIDE = 4
ROWS = 128
STEP = 2
THETA = 500000.0
EPS = 1e-05
HIDDEN_POS = 1 << 30
MIB = 1 << 20


def move(value, step):
    pairs = []
    for y in range(SIDE):
        for x in range(SIDE):
            for z in range(SIDE):
                for core in range(2):
                    ty, tx, tz, tc = step(y, x, z, core)
                    source = ((y * SIDE + x) * SIDE + z) * 2 + core
                    target = (((ty % SIDE) * SIDE + tx % SIDE) * SIDE + tz % SIDE) * 2 + tc
                    pairs.append((source, target))
    return lax.ppermute(value, ("req", "tp"), pairs)


def way(core):
    return 1 if core == 0 else -1


def along_x(value, sign):
    return move(value, lambda y, x, z, c: (y, x + sign * way(c), z, c))


def along_y(value, sign):
    return move(value, lambda y, x, z, c: (y + sign * way(c), x, z, c))


def along_z(value):
    return move(value, lambda y, x, z, c: (y, x, z + way(c), c))


def other_core(value):
    return move(value, lambda y, x, z, c: (y, x, z, 1 - c))


def norm_kernel(tokens_ref, gain_ref, out_ref):
    hidden = tokens_ref[...].astype(F32)
    scale = lax.rsqrt(jnp.mean(hidden * hidden, axis=-1, keepdims=True) + EPS)
    out_ref[...] = (hidden * scale * gain_ref[...].astype(F32)).astype(BF16)


def normalise(tokens, gain):
    return pl.pallas_call(
        norm_kernel,
        out_shape=jax.ShapeDtypeStruct(tokens.shape, BF16),
        compiler_params=pltpu.CompilerParams(vmem_limit_bytes=8 * MIB),
        name="norm",
    )(tokens, gain.reshape(1, -1))


def pick_kernel(index_ref, *refs):
    sources, (k_fwd, k_back, v_fwd, v_back) = refs[:8], refs[8:]
    for tensor, (fwd, back) in enumerate(((k_fwd, k_back), (v_fwd, v_back))):
        for target in range(3):
            for slot in range(4):
                chosen = sources[tensor * 4 + slot][index_ref[tensor * 12 + target * 4 + slot]]
                if target < 2:
                    fwd[target * 4 + slot] = chosen
                else:
                    back[slot] = chosen


def pick(index, keys, values):
    _, tokens, dim = keys[0].shape
    vmem = pl.BlockSpec(memory_space=pltpu.VMEM)
    shapes = [jax.ShapeDtypeStruct((n, tokens, dim), BF16) for n in (8, 4, 8, 4)]
    return pl.pallas_call(
        pick_kernel,
        out_shape=shapes,
        in_specs=[pl.BlockSpec(memory_space=pltpu.SMEM)] + [vmem] * 8,
        out_specs=[vmem] * 4,
        compiler_params=pltpu.CompilerParams(vmem_limit_bytes=10 * MIB),
        cost_estimate=pl.CostEstimate(flops=0, bytes_accessed=6 * MIB, transcendentals=0),
        name="pick",
    )(index, *keys, *values)


def rope(values, cosine, sine):
    return values * cosine + pltpu.roll(values, 64, 1) * sine


def project_kernel(
    place_ref, p0, p1, p2, p3, p4, p5, p6, p7, wq_ref, wk_hbm, wv_hbm, cos_ref, sin_ref,
    q_ref, nk_ref, nv_ref, x_buf, wk_buf, wv_buf, x_sems, w_sems,
):
    step = pl.program_id(0)
    pieces = (p0, p1, p2, p3, p4, p5, p6, p7)
    rows = p0.shape[0]

    def piece_copy(n):
        at = pl.multiple_of(place_ref[n] * rows, 16)
        return pltpu.make_async_copy(pieces[n], x_buf.at[pl.ds(at, rows)], x_sems.at[n])

    k_copy = pltpu.make_async_copy(wk_hbm, wk_buf, w_sems.at[0])
    v_copy = pltpu.make_async_copy(wv_hbm, wv_buf, w_sems.at[1])

    @pl.when(step == 0)
    def _():
        for n in range(8):
            piece_copy(n).start()
        k_copy.start()
        v_copy.start()
        for n in range(8):
            piece_copy(n).wait()

    cosine = cos_ref[...]
    sine = sin_ref[...]

    @pl.when(step < 4)
    def _():
        raw = jnp.dot(x_buf[...], wq_ref[...], preferred_element_type=F32)
        for h in range(2):
            q_ref[h] = rope(raw[:, h * 128 : (h + 1) * 128], cosine, sine).astype(BF16)

    @pl.when(step == 4)
    def _():
        k_copy.wait()
        v_copy.wait()
        new_k = jnp.dot(x_buf[...], wk_buf[...], preferred_element_type=F32).astype(BF16)
        nk_ref[...] = rope(new_k.astype(F32), cosine, sine).astype(BF16)
        nv_ref[...] = jnp.dot(x_buf[...], wv_buf[...], preferred_element_type=F32).astype(BF16)


def project(place, pieces, w_query, w_key, w_value, cosine, sine):
    rows, width = pieces[0].shape
    sel = 8 * rows
    any_spec = pl.BlockSpec(memory_space=pl.ANY)
    whole = pl.BlockSpec((sel, 128), lambda i: (0, 0))
    last = lambda i: jnp.minimum(i, 3)
    return pl.pallas_call(
        project_kernel,
        grid=(5,),
        out_shape=[
            jax.ShapeDtypeStruct((8, sel, 128), BF16),
            jax.ShapeDtypeStruct((sel, 128), BF16),
            jax.ShapeDtypeStruct((sel, 128), BF16),
        ],
        in_specs=[pl.BlockSpec(memory_space=pltpu.SMEM)]
        + [any_spec] * 8
        + [pl.BlockSpec((width, 256), lambda i: (0, last(i))), any_spec, any_spec, whole, whole],
        out_specs=[pl.BlockSpec((2, sel, 128), lambda i: (last(i), 0, 0)), whole, whole],
        scratch_shapes=[
            pltpu.VMEM((sel, width), BF16),
            pltpu.VMEM((width, 128), BF16),
            pltpu.VMEM((width, 128), BF16),
            pltpu.SemaphoreType.DMA((8,)),
            pltpu.SemaphoreType.DMA((2,)),
        ],
        compiler_params=pltpu.CompilerParams(vmem_limit_bytes=24 * MIB),
        cost_estimate=pl.CostEstimate(
            flops=2 * sel * width * 1280, bytes_accessed=30 * MIB, transcendentals=0
        ),
        name="project",
    )(place, *pieces, w_query, w_key, w_value, cosine, sine)


def attend_kernel(
    where_ref, count_ref, q_ref, nk_ref, nv_ref, qpos_ref, kpos_ref, npos_ref, cos_ref, sin_ref, far_cos_ref, far_sin_ref, *refs
):
    keys, values, out_ref = refs[:7], refs[7:14], refs[14]
    k_buf, v_buf, nv_buf, s_buf, m_buf, acc, sems = refs[15:]
    block = k_buf.shape[1]
    blocks = k_buf.shape[0]
    heads, sel, dim = q_ref.shape
    ctx = block * blocks
    tall = heads * ROWS
    factor = 1.4426950408889634 / (dim ** 0.5)

    def k_dest(j):
        return k_buf.at[j]

    def v_dest(j):
        return v_buf.at[pl.ds(j * block, block), pl.ds(0, dim)]

    for j in range(blocks):
        for n in range(7):

            @pl.when(where_ref[0, j] == n)
            def _():
                pltpu.make_async_copy(keys[n].at[where_ref[1, j]], k_dest(j), sems.at[0, j]).start()

            @pl.when(where_ref[2, j] == n)
            def _():
                pltpu.make_async_copy(values[n].at[where_ref[3, j]], v_dest(j), sems.at[1, j]).start()

    v_buf[:, dim:] = jnp.ones((ctx, dim), BF16)
    nv_buf[:, dim:] = jnp.ones((sel, dim), BF16)
    nv_buf[:, :dim] = nv_ref[...]

    for j in range(blocks):
        pltpu.make_async_copy(keys[0].at[0], k_dest(j), sems.at[0, j]).wait()
        far_cos, far_sin = far_cos_ref[j : j + 1, :], far_sin_ref[j : j + 1, :]
        cosine = far_cos * cos_ref[...] - far_sin * sin_ref[...]
        sine = far_sin * cos_ref[...] + far_cos * sin_ref[...]
        k_buf[j] = rope(k_buf[j].astype(F32), cosine, sine).astype(BF16)
    for j in range(blocks):
        pltpu.make_async_copy(values[0].at[0], v_dest(j), sems.at[1, j]).wait()

    def masked_scores(queries, key_block, key_pos, query_pos):
        width = key_block.shape[0]
        scores = lax.dot_general(
            queries, key_block, (((1,), (1,)), ((), ())), preferred_element_type=F32
        )
        reps = width // 128
        seen = key_pos <= jnp.concatenate([query_pos] * reps, axis=1)
        scores = jnp.where(seen[None], scores.reshape(heads, ROWS, width), -jnp.inf)
        scores = scores.reshape(tall, width)
        most = scores[:, :128]
        for n in range(1, reps):
            most = jnp.maximum(most, scores[:, n * 128 : (n + 1) * 128])
        return scores, most

    def tile(i, carry):
        rows = pl.ds(pl.multiple_of(i * ROWS, ROWS), ROWS)
        queries = q_ref[:, rows, :].reshape(tall, dim)
        query_pos = qpos_ref[rows, :]
        scores, most = masked_scores(queries, nk_ref[...], npos_ref[...], query_pos)
        s_buf[:, ctx:] = scores
        m_buf[...] = most
        count = (count_ref[i] + STEP - 1) // STEP
        span = STEP * block

        def first(j, carry):
            scores, most = masked_scores(
                q_ref[:, rows, :].reshape(tall, dim),
                k_buf[pl.ds(j * STEP, STEP)].reshape(span, dim),
                jnp.concatenate([kpos_ref[pl.ds(j * STEP + n, 1), :] for n in range(STEP)], axis=1),
                qpos_ref[rows, :],
            )
            s_buf[:, pl.ds(pl.multiple_of(j * span, span), span)] = scores
            m_buf[...] = jnp.maximum(m_buf[...], most)
            return carry

        lax.fori_loop(0, count, first, 0)
        m_buf[...] = jnp.broadcast_to(jnp.max(m_buf[...], axis=1, keepdims=True), (tall, 128))

        def expos(scores):
            most = jnp.concatenate([m_buf[...]] * (scores.shape[1] // 128), axis=1)
            return jnp.exp2((scores - most) * factor).astype(BF16)

        acc[...] = jnp.dot(expos(s_buf[:, ctx:]), nv_buf[...], preferred_element_type=F32)

        def second(j, carry):
            at = pl.ds(pl.multiple_of(j * span, span), span)
            acc[...] += jnp.dot(expos(s_buf[:, at]), v_buf[at, :], preferred_element_type=F32)
            return carry

        lax.fori_loop(0, count, second, 0)
        result = (acc[:, :dim] / acc[:, dim:]).astype(BF16)
        for h in range(heads):
            out_ref[rows, h * dim : (h + 1) * dim] = result[h * ROWS : (h + 1) * ROWS]
        return carry

    lax.fori_loop(0, sel // ROWS, tile, 0)


def attend(where, count, queries, new_k, new_v, qpos, kpos, npos, angles, keys, values):
    heads, sel, dim = queries.shape
    _, block, _ = keys[0].shape
    blocks = kpos.shape[0]
    ctx = block * blocks
    smem = pl.BlockSpec(memory_space=pltpu.SMEM)
    vmem = pl.BlockSpec(memory_space=pltpu.VMEM)
    any_spec = pl.BlockSpec(memory_space=pl.ANY)
    tall = heads * ROWS
    return pl.pallas_call(
        attend_kernel,
        out_shape=jax.ShapeDtypeStruct((sel, heads * dim), BF16),
        in_specs=[smem] * 2 + [vmem] * 10 + [any_spec] * 14,
        out_specs=vmem,
        scratch_shapes=[
            pltpu.VMEM((blocks, block, dim), BF16),
            pltpu.VMEM((ctx, 2 * dim), BF16),
            pltpu.VMEM((sel, 2 * dim), BF16),
            pltpu.VMEM((tall, ctx + sel), F32),
            pltpu.VMEM((tall, 128), F32),
            pltpu.VMEM((tall, 2 * dim), F32),
            pltpu.SemaphoreType.DMA((2, blocks)),
        ],
        compiler_params=pltpu.CompilerParams(vmem_limit_bytes=40 * MIB),
        cost_estimate=pl.CostEstimate(
            flops=4 * heads * sel * ctx * dim, bytes_accessed=8 * MIB, transcendentals=heads * sel * ctx
        ),
        name="attend",
    )(where, count, queries, new_k, new_v, qpos, kpos, npos, *angles, *keys, *values)


def tables(positions):
    frequency = THETA ** (-(2.0 / 128) * jnp.arange(64).astype(F32))
    angles = positions.astype(F32)[:, None] * frequency[None, :]
    cosine, sine = jnp.cos(angles), jnp.sin(angles)
    return jnp.concatenate([cosine, cosine], axis=1), jnp.concatenate([-sine, sine], axis=1)


def order_of(offset, sign):
    return jnp.where(
        offset == 0, 0, jnp.where(offset == 2, 3, jnp.where(offset == (-sign) % SIDE, 1, 2))
    )


def on_device(
    tokens, norm_gain, w_query, w_key, w_value, store_keys, store_values, block_slot, retrieval, sel_index
):
    held, block, _, dim = store_keys.shape
    requests, chosen_count = retrieval.shape
    stores = block_slot.shape[0] // held
    req, tp = lax.axis_index("req"), lax.axis_index("tp")
    y, x = req // SIDE, req % SIDE
    z, core = tp // 2, tp % 2
    sign = 1 - 2 * core

    own_k = store_keys.reshape(held, block, dim)
    own_v = store_values.reshape(held, block, dim)
    k_one, k_two = along_x(own_k, 1), along_x(own_k, -1)
    v_one, v_two = along_y(own_v, 1), along_y(own_v, -1)
    normed = normalise(tokens[0], norm_gain)
    z_one = along_z(normed)
    k_far, v_far = along_x(k_one, 1), along_y(v_one, 1)
    z_two = along_z(z_one)
    z_far = along_z(z_two)
    mine = [normed, z_one, z_two, z_far]
    theirs = [other_core(piece) for piece in mine]
    row_k = [own_k, k_one, k_two, k_far]
    column_v = [own_v, v_one, v_two, v_far]

    hot = retrieval[:, :, None] == jnp.arange(block_slot.shape[0])[None, None, :]
    slots = jnp.sum(jnp.where(hot, block_slot[None, None, :], 0), axis=2)
    at_store = (slots // held)[:, :, None] == jnp.arange(stores)[None, None, :]
    wanted = jnp.sum(jnp.where(at_store, (slots % held)[:, :, None], 0), axis=1).reshape(-1)
    arrivals = [0, -sign, sign, 2]
    targets = [sign, 2, -sign]

    def node(yy, xx):
        return ((yy + SIDE) % SIDE) * SIDE + (xx + SIDE) % SIDE

    picks = [node(y + t, x) * stores + node(y, x + a) for t in targets for a in arrivals]
    picks += [node(y, x + t) * stores + node(y + a, x) for t in targets for a in arrivals]
    pick_at = jnp.stack(picks)
    entries = pick_at[:, None] == jnp.arange(requests * stores)[None, :]
    index = jnp.sum(jnp.where(entries, wanted[None, :], 0), axis=1).astype(jnp.int32)

    k_fwd, k_back, v_fwd, v_back = pick(index, row_k, column_v)
    k_fwd, k_back = along_y(k_fwd, 1), along_y(k_back, -1)
    v_fwd, v_back = along_x(v_fwd, 1), along_x(v_back, -1)
    k_last, v_last = along_y(k_fwd[4:], 1), along_x(v_fwd[4:], 1)
    keys = row_k + [k_fwd, k_back, k_last]
    values = column_v + [v_fwd, v_back, v_last]

    own_slots = jnp.sum(jnp.where((jnp.arange(requests) == req)[:, None], slots, 0), axis=0)
    store, local = own_slots // held, own_slots % held
    order_y = order_of((store // SIDE - y) % SIDE, sign)
    order_x = order_of((store % SIDE - x) % SIDE, sign)
    where = jnp.stack(
        [
            jnp.where(order_y == 0, order_x, 3 + order_y),
            jnp.where(order_y == 0, local, order_x),
            jnp.where(order_x == 0, order_y, 3 + order_x),
            jnp.where(order_x == 0, local, order_y),
        ]
    ).astype(jnp.int32)

    positions = sel_index[0]
    sel = positions.shape[0]
    ctx = chosen_count * block
    everywhere = jnp.arange(ctx, dtype=jnp.int32)
    replaced = jnp.any(positions[:, None] == everywhere[None, :], axis=0)
    kpos = jnp.where(replaced, HIDDEN_POS, everywhere).reshape(chosen_count, block)
    qpos = jnp.broadcast_to(positions[:, None], (sel, 128))
    count = positions[ROWS - 1 :: ROWS] // block + 1
    q_cos, q_sin = tables(positions)
    angles = (*tables(everywhere[:block]), *tables(everywhere[::block]))

    place = jnp.stack(
        [((z + s * sign + SIDE) % SIDE) * 2 + core for s in (0, -1, 2, 1)]
        + [((z + s * sign + SIDE) % SIDE) * 2 + 1 - core for s in (0, 1, 2, -1)]
    ).astype(jnp.int32)
    queries, new_k, new_v = project(place, mine + theirs, w_query, w_key, w_value, q_cos, q_sin)
    mixed = attend(
        where, count, queries, new_k, new_v, qpos, kpos, positions[None], angles, keys, values
    )
    return mixed[None]


def solution(mesh):
    placed = (
        P("req", "tp", None),
        P(),
        P(None, "tp"),
        P(None, "tp"),
        P(None, "tp"),
        P("req", None, "tp", None),
        P("req", None, "tp", None),
        P(),
        P(),
        P("req", None),
    )
    return jax.shard_map(
        on_device, mesh=mesh, in_specs=placed, out_specs=P("req", None, "tp"), check_vma=False
    )
```

```python
import functools

import jax
import jax.numpy as jnp
from jax import lax
from jax.experimental import pallas as pl
from jax.experimental.pallas import tpu as pltpu
from jax.sharding import PartitionSpec as P

BF16 = jnp.bfloat16
F32 = jnp.float32
SIDE = 4
ROWS = 128
STEP = 2
THETA = 500000.0
EPS = 1e-05
HIDDEN_POS = 1 << 30
MIB = 1 << 20


def move(value, step):
    pairs = []
    for y in range(SIDE):
        for x in range(SIDE):
            for z in range(SIDE):
                for core in range(2):
                    ty, tx, tz, tc = step(y, x, z, core)
                    source = ((y * SIDE + x) * SIDE + z) * 2 + core
                    target = (((ty % SIDE) * SIDE + tx % SIDE) * SIDE + tz % SIDE) * 2 + tc
                    pairs.append((source, target))
    return lax.ppermute(value, ("req", "tp"), pairs)


def first_axis(value, step):
    return move(value, lambda y, x, z, c: (y, x + step, z, c) if c == 0 else (y + step, x, z, c))


def second_axis(value, step):
    return move(value, lambda y, x, z, c: (y + step, x, z, c) if c == 0 else (y, x + step, z, c))


def along_z(value, step):
    return move(value, lambda y, x, z, c: (y, x, z + step, c))


def around_z(value):
    return move(value, lambda y, x, z, c: (y, x, z + 1 - 2 * c, c))


def other_core(value):
    return move(value, lambda y, x, z, c: (y, x, z, 1 - c))


def norm_kernel(tokens_ref, gain_ref, out_ref):
    hidden = tokens_ref[...].astype(F32)
    scale = lax.rsqrt(jnp.mean(hidden * hidden, axis=-1, keepdims=True) + EPS)
    out_ref[...] = (hidden * scale * gain_ref[...].astype(F32)).astype(BF16)


def normalise(tokens, gain):
    return pl.pallas_call(
        norm_kernel,
        out_shape=jax.ShapeDtypeStruct(tokens.shape, BF16),
        compiler_params=pltpu.CompilerParams(vmem_limit_bytes=8 * MIB),
        name="norm",
    )(tokens, gain.reshape(1, -1))


def pick_kernel(index_ref, own, before, behind, k_far, v_far, up, down):
    sources = (own, before, behind)
    held = k_far.shape[0]
    for slot in range(4):
        for target in range(3):
            n = index_ref[target * 4 + slot]
            keys = sources[slot].at[n] if slot < 3 else k_far.at[n]
            values = sources[slot].at[held + n] if slot < 3 else v_far.at[n]
            if target == 0:
                up[slot] = keys[...]
                up[4 + slot] = values[...]
            elif target == 1:
                up[8 + slot] = keys[...]
                down[8 + slot] = values[...]
            else:
                down[slot] = keys[...]
                down[4 + slot] = values[...]


def pick(index, own, before, behind, k_far, v_far):
    _, tokens, dim = own.shape
    vmem = pl.BlockSpec(memory_space=pltpu.VMEM)
    return pl.pallas_call(
        pick_kernel,
        out_shape=[jax.ShapeDtypeStruct((12, tokens, dim), BF16)] * 2,
        in_specs=[pl.BlockSpec(memory_space=pltpu.SMEM)] + [vmem] * 5,
        out_specs=[vmem] * 2,
        compiler_params=pltpu.CompilerParams(vmem_limit_bytes=10 * MIB),
        cost_estimate=pl.CostEstimate(flops=0, bytes_accessed=6 * MIB, transcendentals=0),
        name="pick",
    )(index, own, before, behind, k_far, v_far)


def rope(values, cosine, sine):
    return values * cosine + pltpu.roll(values, 64, 1) * sine


def project_kernel(
    place_ref, p0, p1, p2, p3, near, remote, wq_ref, wk_hbm, wv_hbm, cos_ref, sin_ref,
    q_ref, nk_ref, nv_ref, x_buf, wk_buf, wv_buf, x_sems, w_sems,
):
    step = pl.program_id(0)
    rows = p0.shape[0]
    pieces = [p0, p1, p2, p3] + [ref.at[pl.ds(n * rows, rows)] for ref in (near, remote) for n in range(ref.shape[0] // rows)]

    def piece_copy(n):
        at = pl.multiple_of(place_ref[n] * rows, 16)
        return pltpu.make_async_copy(pieces[n], x_buf.at[pl.ds(at, rows)], x_sems.at[n])

    k_copy = pltpu.make_async_copy(wk_hbm, wk_buf, w_sems.at[0])
    v_copy = pltpu.make_async_copy(wv_hbm, wv_buf, w_sems.at[1])

    @pl.when(step == 0)
    def _():
        for n in range(8):
            piece_copy(n).start()
        k_copy.start()
        v_copy.start()
        for n in range(8):
            piece_copy(n).wait()

    cosine = cos_ref[...]
    sine = sin_ref[...]

    @pl.when(step < 4)
    def _():
        raw = jnp.dot(x_buf[...], wq_ref[...], preferred_element_type=F32)
        for h in range(2):
            q_ref[h] = rope(raw[:, h * 128 : (h + 1) * 128], cosine, sine).astype(BF16)

    @pl.when(step == 4)
    def _():
        k_copy.wait()
        v_copy.wait()
        new_k = jnp.dot(x_buf[...], wk_buf[...], preferred_element_type=F32).astype(BF16)
        nk_ref[...] = rope(new_k.astype(F32), cosine, sine).astype(BF16)
        nv_ref[...] = jnp.dot(x_buf[...], wv_buf[...], preferred_element_type=F32).astype(BF16)


def project(place, pieces, w_query, w_key, w_value, cosine, sine):
    rows, width = pieces[0].shape
    sel = 8 * rows
    any_spec = pl.BlockSpec(memory_space=pl.ANY)
    whole = pl.BlockSpec((sel, 128), lambda i: (0, 0))
    last = lambda i: jnp.minimum(i, 3)
    return pl.pallas_call(
        project_kernel,
        grid=(5,),
        out_shape=[
            jax.ShapeDtypeStruct((8, sel, 128), BF16),
            jax.ShapeDtypeStruct((sel, 128), BF16),
            jax.ShapeDtypeStruct((sel, 128), BF16),
        ],
        in_specs=[pl.BlockSpec(memory_space=pltpu.SMEM)]
        + [any_spec] * 6
        + [pl.BlockSpec((width, 256), lambda i: (0, last(i))), any_spec, any_spec, whole, whole],
        out_specs=[pl.BlockSpec((2, sel, 128), lambda i: (last(i), 0, 0)), whole, whole],
        scratch_shapes=[
            pltpu.VMEM((sel, width), BF16),
            pltpu.VMEM((width, 128), BF16),
            pltpu.VMEM((width, 128), BF16),
            pltpu.SemaphoreType.DMA((8,)),
            pltpu.SemaphoreType.DMA((2,)),
        ],
        compiler_params=pltpu.CompilerParams(vmem_limit_bytes=40 * MIB),
        cost_estimate=pl.CostEstimate(
            flops=2 * sel * width * 1280, bytes_accessed=30 * MIB, transcendentals=0
        ),
        name="project",
    )(place, *pieces, w_query, w_key, w_value, cosine, sine)


def attend_kernel(
    where_ref, count_ref, q_ref, nk_ref, nv_ref, qpos_ref, kpos_ref, npos_ref, cos_ref, sin_ref, far_cos_ref, far_sin_ref, *refs
):
    own, before, behind, k_far, v_far, up, down, k_last, v_last, out_ref = refs[:10]
    k_buf, v_buf, nv_buf, s_buf, m_buf, acc, sems = refs[10:]
    keys = (own, before, behind, k_far, up, down, k_last)
    values = (own, before, behind, v_far, up, down, v_last)
    block = k_buf.shape[1]
    blocks = k_buf.shape[0]
    heads, sel, dim = q_ref.shape
    ctx = block * blocks
    tall = heads * ROWS
    factor = 1.4426950408889634 / (dim ** 0.5)

    def k_dest(j):
        return k_buf.at[j]

    def v_dest(j):
        return v_buf.at[pl.ds(j * block, block), pl.ds(0, dim)]

    for j in range(blocks):
        for n in range(7):

            @pl.when(where_ref[0, j] == n)
            def _():
                pltpu.make_async_copy(keys[n].at[where_ref[1, j]], k_dest(j), sems.at[0, j]).start()

            @pl.when(where_ref[2, j] == n)
            def _():
                pltpu.make_async_copy(values[n].at[where_ref[3, j]], v_dest(j), sems.at[1, j]).start()

    v_buf[:, dim:] = jnp.ones((ctx, dim), BF16)
    nv_buf[:, dim:] = jnp.ones((sel, dim), BF16)
    nv_buf[:, :dim] = nv_ref[...]

    for j in range(blocks):
        pltpu.make_async_copy(keys[0].at[0], k_dest(j), sems.at[0, j]).wait()
        far_cos, far_sin = far_cos_ref[j : j + 1, :], far_sin_ref[j : j + 1, :]
        cosine = far_cos * cos_ref[...] - far_sin * sin_ref[...]
        sine = far_sin * cos_ref[...] + far_cos * sin_ref[...]
        k_buf[j] = rope(k_buf[j].astype(F32), cosine, sine).astype(BF16)
    for j in range(blocks):
        pltpu.make_async_copy(values[0].at[0], v_dest(j), sems.at[1, j]).wait()

    def masked_scores(queries, key_block, key_pos, query_pos):
        width = key_block.shape[0]
        scores = lax.dot_general(
            queries, key_block, (((1,), (1,)), ((), ())), preferred_element_type=F32
        )
        reps = width // 128
        seen = key_pos <= jnp.concatenate([query_pos] * reps, axis=1)
        scores = jnp.where(seen[None], scores.reshape(heads, ROWS, width), -jnp.inf)
        scores = scores.reshape(tall, width)
        most = scores[:, :128]
        for n in range(1, reps):
            most = jnp.maximum(most, scores[:, n * 128 : (n + 1) * 128])
        return scores, most

    def tile(i, carry):
        rows = pl.ds(pl.multiple_of(i * ROWS, ROWS), ROWS)
        queries = q_ref[:, rows, :].reshape(tall, dim)
        query_pos = qpos_ref[rows, :]
        scores, most = masked_scores(queries, nk_ref[...], npos_ref[...], query_pos)
        s_buf[:, ctx:] = scores
        m_buf[...] = most
        count = (count_ref[i] + STEP - 1) // STEP
        span = STEP * block

        def first(j, carry):
            scores, most = masked_scores(
                q_ref[:, rows, :].reshape(tall, dim),
                k_buf[pl.ds(j * STEP, STEP)].reshape(span, dim),
                jnp.concatenate([kpos_ref[pl.ds(j * STEP + n, 1), :] for n in range(STEP)], axis=1),
                qpos_ref[rows, :],
            )
            s_buf[:, pl.ds(pl.multiple_of(j * span, span), span)] = scores
            m_buf[...] = jnp.maximum(m_buf[...], most)
            return carry

        lax.fori_loop(0, count, first, 0)
        m_buf[...] = jnp.broadcast_to(jnp.max(m_buf[...], axis=1, keepdims=True), (tall, 128))

        def expos(scores):
            most = jnp.concatenate([m_buf[...]] * (scores.shape[1] // 128), axis=1)
            return jnp.exp2((scores - most) * factor).astype(BF16)

        acc[...] = jnp.dot(expos(s_buf[:, ctx:]), nv_buf[...], preferred_element_type=F32)

        def second(j, carry):
            at = pl.ds(pl.multiple_of(j * span, span), span)
            acc[...] += jnp.dot(expos(s_buf[:, at]), v_buf[at, :], preferred_element_type=F32)
            return carry

        lax.fori_loop(0, count, second, 0)
        result = (acc[:, :dim] / acc[:, dim:]).astype(BF16)
        for h in range(heads):
            out_ref[rows, h * dim : (h + 1) * dim] = result[h * ROWS : (h + 1) * ROWS]
        return carry

    lax.fori_loop(0, sel // ROWS, tile, 0)


def attend(where, count, queries, new_k, new_v, qpos, kpos, npos, angles, arrays):
    heads, sel, dim = queries.shape
    _, block, _ = arrays[0].shape
    blocks = kpos.shape[0]
    ctx = block * blocks
    smem = pl.BlockSpec(memory_space=pltpu.SMEM)
    vmem = pl.BlockSpec(memory_space=pltpu.VMEM)
    any_spec = pl.BlockSpec(memory_space=pl.ANY)
    tall = heads * ROWS
    return pl.pallas_call(
        attend_kernel,
        out_shape=jax.ShapeDtypeStruct((sel, heads * dim), BF16),
        in_specs=[smem] * 2 + [vmem] * 10 + [any_spec] * 9,
        out_specs=vmem,
        scratch_shapes=[
            pltpu.VMEM((blocks, block, dim), BF16),
            pltpu.VMEM((ctx, 2 * dim), BF16),
            pltpu.VMEM((sel, 2 * dim), BF16),
            pltpu.VMEM((tall, ctx + sel), F32),
            pltpu.VMEM((tall, 128), F32),
            pltpu.VMEM((tall, 2 * dim), F32),
            pltpu.SemaphoreType.DMA((2, blocks)),
        ],
        compiler_params=pltpu.CompilerParams(vmem_limit_bytes=40 * MIB),
        cost_estimate=pl.CostEstimate(
            flops=4 * heads * sel * ctx * dim, bytes_accessed=8 * MIB, transcendentals=heads * sel * ctx
        ),
        name="attend",
    )(where, count, queries, new_k, new_v, qpos, kpos, npos, *angles, *arrays)


def tables(positions):
    frequency = THETA ** (-(2.0 / 128) * jnp.arange(64).astype(F32))
    angles = positions.astype(F32)[:, None] * frequency[None, :]
    cosine, sine = jnp.cos(angles), jnp.sin(angles)
    return jnp.concatenate([cosine, cosine], axis=1), jnp.concatenate([-sine, sine], axis=1)


def order_of(offset):
    return jnp.where(offset == 0, 0, jnp.where(offset == 2, 3, jnp.where(offset == 3, 1, 2)))


def on_device(
    tokens, norm_gain, w_query, w_key, w_value, store_keys, store_values, block_slot, retrieval, sel_index
):
    held, block, _, dim = store_keys.shape
    requests, chosen_count = retrieval.shape
    stores = block_slot.shape[0] // held
    req, tp = lax.axis_index("req"), lax.axis_index("tp")
    y, x = req // SIDE, req % SIDE
    z, core = tp // 2, tp % 2
    own = jnp.concatenate(
        [store_keys.reshape(held, block, dim), store_values.reshape(held, block, dim)]
    )
    before, behind = first_axis(own, 1), first_axis(own, -1)
    normed = normalise(tokens[0], norm_gain)
    z_before, z_behind = along_z(normed, 1), along_z(normed, -1)
    k_far, v_far = first_axis(before[:held], 1), first_axis(behind[held:], -1)
    z_far = around_z(jnp.where(core == 0, z_before, z_behind))
    near = other_core(jnp.concatenate([normed, z_before, z_behind]))
    remote = other_core(z_far)

    hot = retrieval[:, :, None] == jnp.arange(block_slot.shape[0])[None, None, :]
    slots = jnp.sum(jnp.where(hot, block_slot[None, None, :], 0), axis=2)
    at_store = (slots // held)[:, :, None] == jnp.arange(stores)[None, None, :]
    wanted = jnp.sum(jnp.where(at_store, (slots % held)[:, :, None], 0), axis=1).reshape(-1)

    def node(first, second):
        first, second = (first + SIDE) % SIDE, (second + SIDE) % SIDE
        return jnp.where(core == 0, second * SIDE + first, first * SIDE + second)

    first = jnp.where(core == 0, x, y)
    second = jnp.where(core == 0, y, x)
    picks = [
        node(first, second + target) * stores + node(first + arrival, second)
        for target in (1, 2, -1)
        for arrival in (0, -1, 1, 2)
    ]
    pick_at = jnp.stack(picks)
    entries = pick_at[:, None] == jnp.arange(requests * stores)[None, :]
    index = jnp.sum(jnp.where(entries, wanted[None, :], 0), axis=1).astype(jnp.int32)

    up, down = pick(index, own, before, behind, k_far, v_far)
    up, down = second_axis(up, 1), second_axis(down, -1)
    k_last, v_last = second_axis(up[8:], 1), second_axis(down[8:], -1)

    own_slots = jnp.sum(jnp.where((jnp.arange(requests) == req)[:, None], slots, 0), axis=0)
    store, local = own_slots // held, own_slots % held
    store_y, store_x = store // SIDE, store % SIDE
    one = order_of((jnp.where(core == 0, store_x, store_y) - first) % SIDE)
    two = order_of((jnp.where(core == 0, store_y, store_x) - second) % SIDE)
    array = jnp.where(two == 0, one, 3 + two)
    entry = jnp.where(two == 0, local, one)
    offset = jnp.where(two == 0, held, 4)
    shared = (array != 3) & (array != 6)
    where = jnp.stack([array, entry, array, jnp.where(shared, entry + offset, entry)]).astype(jnp.int32)

    positions = sel_index[0]
    sel = positions.shape[0]
    ctx = chosen_count * block
    everywhere = jnp.arange(ctx, dtype=jnp.int32)
    replaced = jnp.any(positions[:, None] == everywhere[None, :], axis=0)
    kpos = jnp.where(replaced, HIDDEN_POS, everywhere).reshape(chosen_count, block)
    qpos = jnp.broadcast_to(positions[:, None], (sel, 128))
    count = positions[ROWS - 1 :: ROWS] // block + 1
    q_cos, q_sin = tables(positions)
    angles = (*tables(everywhere[:block]), *tables(everywhere[::block]))

    place = jnp.stack(
        [((z + s + SIDE) % SIDE) * 2 + core for s in (0, -1, 1, 2)]
        + [((z + s + SIDE) % SIDE) * 2 + 1 - core for s in (0, -1, 1, 2)]
    ).astype(jnp.int32)
    queries, new_k, new_v = project(place, [normed, z_before, z_behind, z_far, near, remote], w_query, w_key, w_value, q_cos, q_sin)
    mixed = attend(
        where, count, queries, new_k, new_v, qpos, kpos, positions[None], angles,
        [own, before, behind, k_far, v_far, up, down, k_last, v_last],
    )
    return mixed[None]


def solution(mesh):
    placed = (
        P("req", "tp", None),
        P(),
        P(None, "tp"),
        P(None, "tp"),
        P(None, "tp"),
        P("req", None, "tp", None),
        P("req", None, "tp", None),
        P(),
        P(),
        P("req", None),
    )
    return jax.shard_map(
        on_device, mesh=mesh, in_specs=placed, out_specs=P("req", None, "tp"), check_vma=False
    )
```

```python
import functools

import jax
import jax.numpy as jnp
from jax import lax
from jax.experimental import pallas as pl
from jax.experimental.pallas import tpu as pltpu
from jax.sharding import PartitionSpec as P

BF16 = jnp.bfloat16
F32 = jnp.float32
SIDE = 4
ROWS = 128
STEP = 2
THETA = 500000.0
EPS = 1e-05
HIDDEN_POS = 1 << 30
MIB = 1 << 20


def move(value, step):
    pairs = []
    for y in range(SIDE):
        for x in range(SIDE):
            for z in range(SIDE):
                for core in range(2):
                    ty, tx, tz, tc = step(y, x, z, core)
                    source = ((y * SIDE + x) * SIDE + z) * 2 + core
                    target = (((ty % SIDE) * SIDE + tx % SIDE) * SIDE + tz % SIDE) * 2 + tc
                    pairs.append((source, target))
    return lax.ppermute(value, ("req", "tp"), pairs)


def first_axis(value, step):
    return move(value, lambda y, x, z, c: (y, x + step, z, c) if c == 0 else (y + step, x, z, c))


def second_axis(value, step):
    return move(value, lambda y, x, z, c: (y + step, x, z, c) if c == 0 else (y, x + step, z, c))


def along_z(value, step):
    return move(value, lambda y, x, z, c: (y, x, z + step, c))


def around_z(value):
    return move(value, lambda y, x, z, c: (y, x, z + 1 - 2 * c, c))


def other_core(value):
    return move(value, lambda y, x, z, c: (y, x, z, 1 - c))


def norm_kernel(tokens_ref, gain_ref, first_ref, out_ref):
    hidden = tokens_ref[...].astype(F32)
    scale = lax.rsqrt(jnp.mean(hidden * hidden, axis=-1, keepdims=True) + EPS)
    out_ref[...] = (hidden * scale * gain_ref[...].astype(F32)).astype(BF16)


def normalise(tokens, gain, first):
    vmem = pl.BlockSpec(memory_space=pltpu.VMEM)
    return pl.pallas_call(
        norm_kernel,
        out_shape=jax.ShapeDtypeStruct(tokens.shape, BF16),
        in_specs=[vmem, vmem, pl.BlockSpec(memory_space=pl.ANY)],
        out_specs=vmem,
        compiler_params=pltpu.CompilerParams(vmem_limit_bytes=8 * MIB),
        name="norm",
    )(tokens, gain.reshape(1, -1), first)


def pick_kernel(index_ref, own, before, behind, k_far, v_far, up, down):
    sources = (own, before, behind)
    held = k_far.shape[0]
    for slot in range(4):
        for target in range(3):
            n = index_ref[target * 4 + slot]
            keys = sources[slot].at[n] if slot < 3 else k_far.at[n]
            values = sources[slot].at[held + n] if slot < 3 else v_far.at[n]
            if target == 0:
                up[slot] = keys[...]
                up[4 + slot] = values[...]
            elif target == 1:
                up[8 + slot] = keys[...]
                down[8 + slot] = values[...]
            else:
                down[slot] = keys[...]
                down[4 + slot] = values[...]


def pick(index, own, before, behind, k_far, v_far):
    _, tokens, dim = own.shape
    vmem = pl.BlockSpec(memory_space=pltpu.VMEM)
    return pl.pallas_call(
        pick_kernel,
        out_shape=[jax.ShapeDtypeStruct((12, tokens, dim), BF16)] * 2,
        in_specs=[pl.BlockSpec(memory_space=pltpu.SMEM)] + [vmem] * 5,
        out_specs=[vmem] * 2,
        compiler_params=pltpu.CompilerParams(vmem_limit_bytes=10 * MIB),
        cost_estimate=pl.CostEstimate(flops=0, bytes_accessed=6 * MIB, transcendentals=0),
        name="pick",
    )(index, own, before, behind, k_far, v_far)


def rope(values, cosine, sine):
    return values * cosine + pltpu.roll(values, 64, 1) * sine


def project_kernel(with_kv, *refs):
    place_ref, p0, p1, p2, p3, near, remote = refs[:7]
    if with_kv:
        wq_ref, wk_hbm, wv_hbm, cos_ref, sin_ref, q_ref, nk_ref, nv_ref = refs[7:15]
        x_buf, x_sems, wk_buf, wv_buf, w_sems = refs[15:]
        k_copy = pltpu.make_async_copy(wk_hbm, wk_buf, w_sems.at[0])
        v_copy = pltpu.make_async_copy(wv_hbm, wv_buf, w_sems.at[1])
    else:
        wq_ref, cos_ref, sin_ref, q_ref, x_buf, x_sems = refs[7:]
    step = pl.program_id(0)
    rows = p0.shape[0]
    pieces = [p0, p1, p2, p3]
    pieces += [ref.at[pl.ds(n * rows, rows)] for ref in (near, remote) for n in range(ref.shape[0] // rows)]

    def piece_copy(n):
        at = pl.multiple_of(place_ref[n] * rows, 16)
        return pltpu.make_async_copy(pieces[n], x_buf.at[pl.ds(at, rows)], x_sems.at[n])

    @pl.when(step == 0)
    def _():
        for n in range(8):
            piece_copy(n).start()
        if with_kv:
            k_copy.start()
            v_copy.start()
        for n in range(8):
            piece_copy(n).wait()

    cosine = cos_ref[...]
    sine = sin_ref[...]

    @pl.when(step < 2)
    def _():
        raw = jnp.dot(x_buf[...], wq_ref[...], preferred_element_type=F32)
        for h in range(2):
            q_ref[h] = rope(raw[:, h * 128 : (h + 1) * 128], cosine, sine).astype(BF16)

    if with_kv:

        @pl.when(step == 2)
        def _():
            k_copy.wait()
            v_copy.wait()
            new_k = jnp.dot(x_buf[...], wk_buf[...], preferred_element_type=F32).astype(BF16)
            nk_ref[...] = rope(new_k.astype(F32), cosine, sine).astype(BF16)
            nv_ref[...] = jnp.dot(x_buf[...], wv_buf[...], preferred_element_type=F32).astype(BF16)


def project(place, pieces, half, w_query, w_kv, cosine, sine):
    rows, width = pieces[0].shape
    sel = 8 * rows
    any_spec = pl.BlockSpec(memory_space=pl.ANY)
    whole = pl.BlockSpec((sel, 128), lambda i: (0, 0))
    last = lambda i: jnp.minimum(i, 1)
    new = [jax.ShapeDtypeStruct((sel, 128), BF16)] * len(w_kv)
    scratch = [pltpu.VMEM((sel, width), BF16), pltpu.SemaphoreType.DMA((8,))]
    if w_kv:
        scratch += [pltpu.VMEM((width, 128), BF16)] * 2 + [pltpu.SemaphoreType.DMA((2,))]
    return pl.pallas_call(
        functools.partial(project_kernel, bool(w_kv)),
        grid=(3 if w_kv else 2,),
        out_shape=[jax.ShapeDtypeStruct((4, sel, 128), BF16)] + new,
        in_specs=[pl.BlockSpec(memory_space=pltpu.SMEM)]
        + [any_spec] * 6
        + [pl.BlockSpec((width, 256), lambda i: (0, 2 * half + last(i)))]
        + [any_spec] * len(w_kv)
        + [whole, whole],
        out_specs=[pl.BlockSpec((2, sel, 128), lambda i: (last(i), 0, 0))] + [whole] * len(w_kv),
        scratch_shapes=scratch,
        compiler_params=pltpu.CompilerParams(vmem_limit_bytes=40 * MIB),
        cost_estimate=pl.CostEstimate(
            flops=0, bytes_accessed=MIB, transcendentals=0
        ),
        name="project",
    )(place, *pieces, w_query, *w_kv, cosine, sine)


def attend_kernel(
    where_ref, count_ref, low_ref, high_ref, nk_ref, nv_ref, qpos_ref, kpos_ref, npos_ref, cos_ref, sin_ref, far_cos_ref, far_sin_ref, *refs
):
    own, before, behind, k_far, v_far, up, down, k_last, v_last, out_ref = refs[:10]
    k_buf, v_buf, nv_buf, q_buf, s_buf, m_buf, acc, sems = refs[10:]
    keys = (own, before, behind, k_far, up, down, k_last)
    values = (own, before, behind, v_far, up, down, v_last)
    block = k_buf.shape[1]
    blocks = k_buf.shape[0]
    heads, sel, dim = 2 * low_ref.shape[0], *low_ref.shape[1:]
    ctx = block * blocks
    tall = heads * ROWS
    factor = 1.4426950408889634 / (dim ** 0.5)

    def k_dest(j):
        return k_buf.at[j]

    def v_dest(j):
        return v_buf.at[pl.ds(j * block, block), pl.ds(0, dim)]

    for j in range(blocks):
        for n in range(7):

            @pl.when(where_ref[0, j] == n)
            def _():
                pltpu.make_async_copy(keys[n].at[where_ref[1, j]], k_dest(j), sems.at[0, j]).start()

            @pl.when(where_ref[2, j] == n)
            def _():
                pltpu.make_async_copy(values[n].at[where_ref[3, j]], v_dest(j), sems.at[1, j]).start()

    v_buf[:, dim:] = jnp.ones((ctx, dim), BF16)
    nv_buf[:, dim:] = jnp.ones((sel, dim), BF16)
    nv_buf[:, :dim] = nv_ref[...]

    for j in range(blocks):
        pltpu.make_async_copy(keys[0].at[0], k_dest(j), sems.at[0, j]).wait()
        far_cos, far_sin = far_cos_ref[j : j + 1, :], far_sin_ref[j : j + 1, :]
        cosine = far_cos * cos_ref[...] - far_sin * sin_ref[...]
        sine = far_sin * cos_ref[...] + far_cos * sin_ref[...]
        k_buf[j] = rope(k_buf[j].astype(F32), cosine, sine).astype(BF16)
    for j in range(blocks):
        pltpu.make_async_copy(values[0].at[0], v_dest(j), sems.at[1, j]).wait()

    def masked_scores(queries, key_block, key_pos, query_pos):
        width = key_block.shape[0]
        scores = lax.dot_general(
            queries, key_block, (((1,), (1,)), ((), ())), preferred_element_type=F32
        )
        reps = width // 128
        seen = key_pos <= jnp.concatenate([query_pos] * reps, axis=1)
        scores = jnp.where(seen[None], scores.reshape(heads, ROWS, width), -jnp.inf)
        scores = scores.reshape(tall, width)
        most = scores[:, :128]
        for n in range(1, reps):
            most = jnp.maximum(most, scores[:, n * 128 : (n + 1) * 128])
        return scores, most

    def tile(i, carry):
        rows = pl.ds(pl.multiple_of(i * ROWS, ROWS), ROWS)
        half = tall // 2
        q_buf[:half] = low_ref[:, rows, :].reshape(half, dim)
        q_buf[half:] = high_ref[:, rows, :].reshape(half, dim)
        queries = q_buf[...]
        query_pos = qpos_ref[rows, :]
        scores, most = masked_scores(queries, nk_ref[...], npos_ref[...], query_pos)
        s_buf[:, ctx:] = scores
        m_buf[...] = most
        count = (count_ref[i] + STEP - 1) // STEP
        span = STEP * block

        def first(j, carry):
            scores, most = masked_scores(
                q_buf[...],
                k_buf[pl.ds(j * STEP, STEP)].reshape(span, dim),
                jnp.concatenate([kpos_ref[pl.ds(j * STEP + n, 1), :] for n in range(STEP)], axis=1),
                qpos_ref[rows, :],
            )
            s_buf[:, pl.ds(pl.multiple_of(j * span, span), span)] = scores
            m_buf[...] = jnp.maximum(m_buf[...], most)
            return carry

        lax.fori_loop(0, count, first, 0)
        m_buf[...] = jnp.broadcast_to(jnp.max(m_buf[...], axis=1, keepdims=True), (tall, 128))

        def expos(scores):
            most = jnp.concatenate([m_buf[...]] * (scores.shape[1] // 128), axis=1)
            return jnp.exp2((scores - most) * factor).astype(BF16)

        acc[...] = jnp.dot(expos(s_buf[:, ctx:]), nv_buf[...], preferred_element_type=F32)

        def second(j, carry):
            at = pl.ds(pl.multiple_of(j * span, span), span)
            acc[...] += jnp.dot(expos(s_buf[:, at]), v_buf[at, :], preferred_element_type=F32)
            return carry

        lax.fori_loop(0, count, second, 0)
        result = (acc[:, :dim] / acc[:, dim:]).astype(BF16)
        for h in range(heads):
            out_ref[rows, h * dim : (h + 1) * dim] = result[h * ROWS : (h + 1) * ROWS]
        return carry

    lax.fori_loop(0, sel // ROWS, tile, 0)


def attend(where, count, low, high, new_k, new_v, qpos, kpos, npos, angles, arrays):
    heads, sel, dim = 2 * low.shape[0], *low.shape[1:]
    _, block, _ = arrays[0].shape
    blocks = kpos.shape[0]
    ctx = block * blocks
    smem = pl.BlockSpec(memory_space=pltpu.SMEM)
    vmem = pl.BlockSpec(memory_space=pltpu.VMEM)
    any_spec = pl.BlockSpec(memory_space=pl.ANY)
    tall = heads * ROWS
    return pl.pallas_call(
        attend_kernel,
        out_shape=jax.ShapeDtypeStruct((sel, heads * dim), BF16),
        in_specs=[smem] * 2 + [vmem] * 11 + [any_spec] * 9,
        out_specs=vmem,
        scratch_shapes=[
            pltpu.VMEM((blocks, block, dim), BF16),
            pltpu.VMEM((ctx, 2 * dim), BF16),
            pltpu.VMEM((sel, 2 * dim), BF16),
            pltpu.VMEM((tall, dim), BF16),
            pltpu.VMEM((tall, ctx + sel), F32),
            pltpu.VMEM((tall, 128), F32),
            pltpu.VMEM((tall, 2 * dim), F32),
            pltpu.SemaphoreType.DMA((2, blocks)),
        ],
        compiler_params=pltpu.CompilerParams(vmem_limit_bytes=40 * MIB),
        cost_estimate=pl.CostEstimate(
            flops=4 * heads * sel * ctx * dim, bytes_accessed=8 * MIB, transcendentals=heads * sel * ctx
        ),
        name="attend",
    )(where, count, low, high, new_k, new_v, qpos, kpos, npos, *angles, *arrays)


def tables(positions):
    frequency = THETA ** (-(2.0 / 128) * jnp.arange(64).astype(F32))
    angles = positions.astype(F32)[:, None] * frequency[None, :]
    cosine, sine = jnp.cos(angles), jnp.sin(angles)
    return jnp.concatenate([cosine, cosine], axis=1), jnp.concatenate([-sine, sine], axis=1)


def order_of(offset):
    return jnp.where(offset == 0, 0, jnp.where(offset == 2, 3, jnp.where(offset == 3, 1, 2)))


def on_device(
    tokens, norm_gain, w_query, w_key, w_value, store_keys, store_values, block_slot, retrieval, sel_index
):
    held, block, _, dim = store_keys.shape
    requests, chosen_count = retrieval.shape
    stores = block_slot.shape[0] // held
    req, tp = lax.axis_index("req"), lax.axis_index("tp")
    y, x = req // SIDE, req % SIDE
    z, core = tp // 2, tp % 2
    own = jnp.concatenate(
        [store_keys.reshape(held, block, dim), store_values.reshape(held, block, dim)]
    )
    before, behind = first_axis(own, 1), first_axis(own, -1)
    normed = normalise(tokens[0], norm_gain, own)
    z_before, z_behind = along_z(normed, 1), along_z(normed, -1)
    k_half, v_half = before[:held], behind[held:]
    k_far, v_far = first_axis(k_half, 1), first_axis(v_half, -1)
    z_before, z_behind, _, _ = lax.optimization_barrier((z_before, z_behind, k_half, v_half))
    z_far = around_z(jnp.where(core == 0, z_before, z_behind))
    near = other_core(jnp.concatenate([normed, z_before, z_behind]))
    remote = other_core(z_far)

    hot = retrieval[:, :, None] == jnp.arange(block_slot.shape[0])[None, None, :]
    slots = jnp.sum(jnp.where(hot, block_slot[None, None, :], 0), axis=2)
    at_store = (slots // held)[:, :, None] == jnp.arange(stores)[None, None, :]
    wanted = jnp.sum(jnp.where(at_store, (slots % held)[:, :, None], 0), axis=1).reshape(-1)

    def node(first, second):
        first, second = (first + SIDE) % SIDE, (second + SIDE) % SIDE
        return jnp.where(core == 0, second * SIDE + first, first * SIDE + second)

    first = jnp.where(core == 0, x, y)
    second = jnp.where(core == 0, y, x)
    picks = [
        node(first, second + target) * stores + node(first + arrival, second)
        for target in (1, 2, -1)
        for arrival in (0, -1, 1, 2)
    ]
    pick_at = jnp.stack(picks)
    entries = pick_at[:, None] == jnp.arange(requests * stores)[None, :]
    index = jnp.sum(jnp.where(entries, wanted[None, :], 0), axis=1).astype(jnp.int32)

    up, down = pick(index, own, before, behind, k_far, v_far)
    up, down = second_axis(up, 1), second_axis(down, -1)

    own_slots = jnp.sum(jnp.where((jnp.arange(requests) == req)[:, None], slots, 0), axis=0)
    store, local = own_slots // held, own_slots % held
    store_y, store_x = store // SIDE, store % SIDE
    one = order_of((jnp.where(core == 0, store_x, store_y) - first) % SIDE)
    two = order_of((jnp.where(core == 0, store_y, store_x) - second) % SIDE)
    array = jnp.where(two == 0, one, 3 + two)
    entry = jnp.where(two == 0, local, one)
    offset = jnp.where(two == 0, held, 4)
    shared = (array != 3) & (array != 6)
    where = jnp.stack([array, entry, array, jnp.where(shared, entry + offset, entry)]).astype(jnp.int32)

    positions = sel_index[0]
    sel = positions.shape[0]
    ctx = chosen_count * block
    everywhere = jnp.arange(ctx, dtype=jnp.int32)
    replaced = jnp.any(positions[:, None] == everywhere[None, :], axis=0)
    kpos = jnp.where(replaced, HIDDEN_POS, everywhere).reshape(chosen_count, block)
    qpos = jnp.broadcast_to(positions[:, None], (sel, 128))
    count = positions[ROWS - 1 :: ROWS] // block + 1
    q_cos, q_sin = tables(positions)
    angles = (*tables(everywhere[:block]), *tables(everywhere[::block]))

    place = jnp.stack(
        [((z + s + SIDE) % SIDE) * 2 + core for s in (0, -1, 1, 2)]
        + [((z + s + SIDE) % SIDE) * 2 + 1 - core for s in (0, -1, 1, 2)]
    ).astype(jnp.int32)
    pieces = [normed, z_before, z_behind, z_far, near, remote]
    low, new_k, new_v = project(place, pieces, 0, w_query, (w_key, w_value), q_cos, q_sin)
    up_first, down_first, _ = lax.optimization_barrier((up, down, low))
    k_last, v_last = second_axis(up_first[8:], 1), second_axis(down_first[8:], -1)
    (high,) = project(place, pieces, 1, w_query, (), q_cos, q_sin)
    mixed = attend(
        where, count, low, high, new_k, new_v, qpos, kpos, positions[None], angles,
        [own, before, behind, k_far, v_far, up, down, k_last, v_last],
    )
    return mixed[None]


def solution(mesh):
    placed = (
        P("req", "tp", None),
        P(),
        P(None, "tp"),
        P(None, "tp"),
        P(None, "tp"),
        P("req", None, "tp", None),
        P("req", None, "tp", None),
        P(),
        P(),
        P("req", None),
    )
    return jax.shard_map(
        on_device, mesh=mesh, in_specs=placed, out_specs=P("req", None, "tp"), check_vma=False
    )
```

```python
import functools

import jax
import jax.numpy as jnp
from jax import lax
from jax.experimental import pallas as pl
from jax.experimental.pallas import tpu as pltpu
from jax.sharding import PartitionSpec as P

BF16 = jnp.bfloat16
F32 = jnp.float32
SIDE = 4
ROWS = 128
STEP = 2
THETA = 500000.0
EPS = 1e-05
HIDDEN_POS = 1 << 30
MIB = 1 << 20


def move(value, step):
    pairs = []
    for y in range(SIDE):
        for x in range(SIDE):
            for z in range(SIDE):
                for core in range(2):
                    ty, tx, tz, tc = step(y, x, z, core)
                    source = ((y * SIDE + x) * SIDE + z) * 2 + core
                    target = (((ty % SIDE) * SIDE + tx % SIDE) * SIDE + tz % SIDE) * 2 + tc
                    pairs.append((source, target))
    return lax.ppermute(value, ("req", "tp"), pairs)


def first_axis(value, step):
    return move(value, lambda y, x, z, c: (y, x + step, z, c) if c == 0 else (y + step, x, z, c))


def second_axis(value, step):
    return move(value, lambda y, x, z, c: (y + step, x, z, c) if c == 0 else (y, x + step, z, c))


def along_z(value, step):
    return move(value, lambda y, x, z, c: (y, x, z + step, c))


def around_z(value):
    return move(value, lambda y, x, z, c: (y, x, z + 1 - 2 * c, c))


def other_core(value):
    return move(value, lambda y, x, z, c: (y, x, z, 1 - c))


def norm_kernel(tokens_ref, gain_ref, first_ref, out_ref):
    hidden = tokens_ref[...].astype(F32)
    scale = lax.rsqrt(jnp.mean(hidden * hidden, axis=-1, keepdims=True) + EPS)
    out_ref[...] = (hidden * scale * gain_ref[...].astype(F32)[None, :]).astype(BF16)


def normalise(tokens, gain, first):
    vmem = pl.BlockSpec(memory_space=pltpu.VMEM)
    return pl.pallas_call(
        norm_kernel,
        out_shape=jax.ShapeDtypeStruct(tokens.shape, BF16),
        in_specs=[vmem, vmem, pl.BlockSpec(memory_space=pl.ANY)],
        out_specs=vmem,
        compiler_params=pltpu.CompilerParams(vmem_limit_bytes=8 * MIB),
        name="norm",
    )(tokens, gain, first)


def pick_kernel(index_ref, own, before, behind, k_far, v_far, up, down):
    sources = (own, before, behind)
    held = k_far.shape[0]
    for slot in range(4):
        for target in range(3):
            n = index_ref[target * 4 + slot]
            keys = sources[slot].at[n] if slot < 3 else k_far.at[n]
            values = sources[slot].at[held + n] if slot < 3 else v_far.at[n]
            if target == 0:
                up[slot] = keys[...]
                up[4 + slot] = values[...]
            elif target == 1:
                up[8 + slot] = keys[...]
                down[8 + slot] = values[...]
            else:
                down[slot] = keys[...]
                down[4 + slot] = values[...]


def pick(index, own, before, behind, k_far, v_far):
    _, tokens, dim = own.shape
    vmem = pl.BlockSpec(memory_space=pltpu.VMEM)
    return pl.pallas_call(
        pick_kernel,
        out_shape=[jax.ShapeDtypeStruct((12, tokens, dim), BF16)] * 2,
        in_specs=[pl.BlockSpec(memory_space=pltpu.SMEM)] + [vmem] * 5,
        out_specs=[vmem] * 2,
        compiler_params=pltpu.CompilerParams(vmem_limit_bytes=10 * MIB),
        cost_estimate=pl.CostEstimate(flops=0, bytes_accessed=6 * MIB, transcendentals=0),
        name="pick",
    )(index, own, before, behind, k_far, v_far)


def rope(values, cosine, sine):
    return values * cosine + pltpu.roll(values, 64, 1) * sine


def project_kernel(with_kv, *refs):
    place_ref, p0, p1, p2, p3, near, remote = refs[:7]
    if with_kv:
        wq_ref, wk_hbm, wv_hbm, cos_ref, sin_ref, q_ref, nk_ref, nv_ref = refs[7:15]
        x_buf, x_sems, wk_buf, wv_buf, w_sems = refs[15:]
        k_copy = pltpu.make_async_copy(wk_hbm, wk_buf, w_sems.at[0])
        v_copy = pltpu.make_async_copy(wv_hbm, wv_buf, w_sems.at[1])
    else:
        wq_ref, cos_ref, sin_ref, q_ref, x_buf, x_sems = refs[7:]
    step = pl.program_id(0)
    rows = p0.shape[0]
    pieces = [p0, p1, p2, p3]
    pieces += [ref.at[pl.ds(n * rows, rows)] for ref in (near, remote) for n in range(ref.shape[0] // rows)]

    def piece_copy(n):
        at = pl.multiple_of(place_ref[n] * rows, 16)
        return pltpu.make_async_copy(pieces[n], x_buf.at[pl.ds(at, rows)], x_sems.at[n])

    @pl.when(step == 0)
    def _():
        for n in range(8):
            piece_copy(n).start()
        if with_kv:
            k_copy.start()
            v_copy.start()
        for n in range(8):
            piece_copy(n).wait()

    cosine = cos_ref[...]
    sine = sin_ref[...]

    @pl.when(step < 2)
    def _():
        raw = jnp.dot(x_buf[...], wq_ref[...], preferred_element_type=F32)
        for h in range(2):
            q_ref[h] = rope(raw[:, h * 128 : (h + 1) * 128], cosine, sine).astype(BF16)

    if with_kv:

        @pl.when(step == 2)
        def _():
            k_copy.wait()
            v_copy.wait()
            new_k = jnp.dot(x_buf[...], wk_buf[...], preferred_element_type=F32).astype(BF16)
            nk_ref[...] = rope(new_k.astype(F32), cosine, sine).astype(BF16)
            nv_ref[...] = jnp.dot(x_buf[...], wv_buf[...], preferred_element_type=F32).astype(BF16)


def project(place, pieces, half, w_query, w_kv, cosine, sine):
    rows, width = pieces[0].shape
    sel = 8 * rows
    any_spec = pl.BlockSpec(memory_space=pl.ANY)
    whole = pl.BlockSpec((sel, 128), lambda i: (0, 0))
    last = lambda i: jnp.minimum(i, 1)
    new = [jax.ShapeDtypeStruct((sel, 128), BF16)] * len(w_kv)
    scratch = [pltpu.VMEM((sel, width), BF16), pltpu.SemaphoreType.DMA((8,))]
    if w_kv:
        scratch += [pltpu.VMEM((width, 128), BF16)] * 2 + [pltpu.SemaphoreType.DMA((2,))]
    return pl.pallas_call(
        functools.partial(project_kernel, bool(w_kv)),
        grid=(3 if w_kv else 2,),
        out_shape=[jax.ShapeDtypeStruct((4, sel, 128), BF16)] + new,
        in_specs=[pl.BlockSpec(memory_space=pltpu.SMEM)]
        + [any_spec] * 6
        + [pl.BlockSpec((width, 256), lambda i: (0, 2 * half + last(i)))]
        + [any_spec] * len(w_kv)
        + [whole, whole],
        out_specs=[pl.BlockSpec((2, sel, 128), lambda i: (last(i), 0, 0))] + [whole] * len(w_kv),
        scratch_shapes=scratch,
        compiler_params=pltpu.CompilerParams(vmem_limit_bytes=40 * MIB),
        cost_estimate=pl.CostEstimate(
            flops=0, bytes_accessed=MIB, transcendentals=0
        ),
        name="project",
    )(place, *pieces, w_query, *w_kv, cosine, sine)


def attend_kernel(
    where_ref, count_ref, low_ref, high_ref, nk_ref, nv_ref, qpos_ref, kpos_ref, npos_ref, cos_ref, sin_ref, far_cos_ref, far_sin_ref, *refs
):
    own, before, behind, k_far, v_far, up, down, k_last, v_last, out_ref = refs[:10]
    k_buf, v_buf, nv_buf, q_buf, s_buf, m_buf, acc, sems = refs[10:]
    keys = (own, before, behind, k_far, up, down, k_last)
    values = (own, before, behind, v_far, up, down, v_last)
    block = k_buf.shape[1]
    blocks = k_buf.shape[0]
    heads, sel, dim = 2 * low_ref.shape[0], *low_ref.shape[1:]
    ctx = block * blocks
    tall = heads * ROWS
    factor = 1.4426950408889634 / (dim ** 0.5)

    def k_dest(j):
        return k_buf.at[j]

    def v_dest(j):
        return v_buf.at[pl.ds(j * block, block), pl.ds(0, dim)]

    for j in range(blocks):
        for n in range(7):

            @pl.when(where_ref[0, j] == n)
            def _():
                pltpu.make_async_copy(keys[n].at[where_ref[1, j]], k_dest(j), sems.at[0, j]).start()
                pltpu.make_async_copy(values[n].at[where_ref[2, j]], v_dest(j), sems.at[1, j]).start()

    v_buf[:, dim:] = jnp.ones((ctx, dim), BF16)
    nv_buf[:, dim:] = jnp.ones((sel, dim), BF16)
    nv_buf[:, :dim] = nv_ref[...]

    for j in range(blocks):
        pltpu.make_async_copy(keys[0].at[0], k_dest(j), sems.at[0, j]).wait()
        far_cos, far_sin = far_cos_ref[j : j + 1, :], far_sin_ref[j : j + 1, :]
        cosine = far_cos * cos_ref[...] - far_sin * sin_ref[...]
        sine = far_sin * cos_ref[...] + far_cos * sin_ref[...]
        k_buf[j] = rope(k_buf[j].astype(F32), cosine, sine).astype(BF16)
    for j in range(blocks):
        pltpu.make_async_copy(values[0].at[0], v_dest(j), sems.at[1, j]).wait()

    def masked_scores(queries, key_block, key_pos, query_pos):
        width = key_block.shape[0]
        scores = lax.dot_general(
            queries, key_block, (((1,), (1,)), ((), ())), preferred_element_type=F32
        )
        reps = width // 128
        seen = key_pos <= jnp.concatenate([query_pos] * reps, axis=1)
        scores = jnp.where(seen[None], scores.reshape(heads, ROWS, width), -jnp.inf)
        scores = scores.reshape(tall, width)
        most = scores[:, :128]
        for n in range(1, reps):
            most = jnp.maximum(most, scores[:, n * 128 : (n + 1) * 128])
        return scores, most

    def tile(i, carry):
        rows = pl.ds(pl.multiple_of(i * ROWS, ROWS), ROWS)
        half = tall // 2
        q_buf[:half] = low_ref[:, rows, :].reshape(half, dim)
        q_buf[half:] = high_ref[:, rows, :].reshape(half, dim)
        queries = q_buf[...]
        query_pos = qpos_ref[rows, :]
        scores, most = masked_scores(queries, nk_ref[...], npos_ref[...], query_pos)
        s_buf[:, ctx:] = scores
        m_buf[...] = most
        count = count_ref[i]

        def first(at, blocks_now):
            span = blocks_now * block
            scores, most = masked_scores(
                q_buf[...],
                k_buf[pl.ds(at, blocks_now)].reshape(span, dim),
                jnp.concatenate([kpos_ref[pl.ds(at + n, 1), :] for n in range(blocks_now)], axis=1),
                qpos_ref[rows, :],
            )
            s_buf[:, pl.ds(pl.multiple_of(at * block, block), span)] = scores
            m_buf[...] = jnp.maximum(m_buf[...], most)

        def over_blocks(body):
            def some(j, carry):
                body(j * STEP, STEP)
                return carry

            lax.fori_loop(0, count // STEP, some, 0)

            @pl.when(count % STEP == 1)
            def _():
                body(count - 1, 1)

        over_blocks(first)
        m_buf[...] = jnp.broadcast_to(jnp.max(m_buf[...], axis=1, keepdims=True), (tall, 128))

        def expos(scores):
            most = jnp.concatenate([m_buf[...]] * (scores.shape[1] // 128), axis=1)
            return jnp.exp2((scores - most) * factor).astype(BF16)

        acc[...] = jnp.dot(expos(s_buf[:, ctx:]), nv_buf[...], preferred_element_type=F32)

        def second(at, blocks_now):
            span = pl.ds(pl.multiple_of(at * block, block), blocks_now * block)
            acc[...] += jnp.dot(expos(s_buf[:, span]), v_buf[span, :], preferred_element_type=F32)

        over_blocks(second)
        result = (acc[:, :dim] / acc[:, dim:]).astype(BF16)
        for h in range(heads):
            out_ref[rows, h * dim : (h + 1) * dim] = result[h * ROWS : (h + 1) * ROWS]
        return carry

    lax.fori_loop(0, sel // ROWS, tile, 0)


def attend(where, count, low, high, new_k, new_v, qpos, kpos, npos, angles, arrays):
    heads, sel, dim = 2 * low.shape[0], *low.shape[1:]
    _, block, _ = arrays[0].shape
    blocks = kpos.shape[0]
    ctx = block * blocks
    smem = pl.BlockSpec(memory_space=pltpu.SMEM)
    vmem = pl.BlockSpec(memory_space=pltpu.VMEM)
    any_spec = pl.BlockSpec(memory_space=pl.ANY)
    tall = heads * ROWS
    return pl.pallas_call(
        attend_kernel,
        out_shape=jax.ShapeDtypeStruct((sel, heads * dim), BF16),
        in_specs=[smem] * 2 + [vmem] * 11 + [any_spec] * 9,
        out_specs=vmem,
        scratch_shapes=[
            pltpu.VMEM((blocks, block, dim), BF16),
            pltpu.VMEM((ctx, 2 * dim), BF16),
            pltpu.VMEM((sel, 2 * dim), BF16),
            pltpu.VMEM((tall, dim), BF16),
            pltpu.VMEM((tall, ctx + sel), F32),
            pltpu.VMEM((tall, 128), F32),
            pltpu.VMEM((tall, 2 * dim), F32),
            pltpu.SemaphoreType.DMA((2, blocks)),
        ],
        compiler_params=pltpu.CompilerParams(vmem_limit_bytes=40 * MIB),
        cost_estimate=pl.CostEstimate(
            flops=4 * heads * sel * ctx * dim, bytes_accessed=8 * MIB, transcendentals=heads * sel * ctx
        ),
        name="attend",
    )(where, count, low, high, new_k, new_v, qpos, kpos, npos, *angles, *arrays)


def tables(positions):
    frequency = THETA ** (-(2.0 / 128) * jnp.arange(64).astype(F32))
    angles = positions.astype(F32)[:, None] * frequency[None, :]
    cosine, sine = jnp.cos(angles), jnp.sin(angles)
    return jnp.concatenate([cosine, cosine], axis=1), jnp.concatenate([-sine, sine], axis=1)


def order_of(offset):
    return jnp.where(offset == 0, 0, jnp.where(offset == 2, 3, jnp.where(offset == 3, 1, 2)))


def on_device(
    tokens, norm_gain, w_query, w_key, w_value, store_keys, store_values, block_slot, retrieval, sel_index
):
    held, block, _, dim = store_keys.shape
    requests, chosen_count = retrieval.shape
    stores = block_slot.shape[0] // held
    req, tp = lax.axis_index("req"), lax.axis_index("tp")
    y, x = req // SIDE, req % SIDE
    z, core = tp // 2, tp % 2
    own = jnp.concatenate(
        [store_keys.reshape(held, block, dim), store_values.reshape(held, block, dim)]
    )
    before, behind = first_axis(own, 1), first_axis(own, -1)
    normed = normalise(tokens[0], norm_gain, own)
    z_before, z_behind = along_z(normed, 1), along_z(normed, -1)
    k_half, v_half = before[:held], behind[held:]
    k_far, v_far = first_axis(k_half, 1), first_axis(v_half, -1)
    z_before, z_behind, _, _ = lax.optimization_barrier((z_before, z_behind, k_half, v_half))
    z_far = around_z(jnp.where(core == 0, z_before, z_behind))
    near = other_core(jnp.concatenate([normed, z_before, z_behind]))
    remote = other_core(z_far)

    hot = retrieval[:, :, None] == jnp.arange(block_slot.shape[0])[None, None, :]
    slots = jnp.sum(jnp.where(hot, block_slot[None, None, :], 0), axis=2)
    at_store = (slots // held)[:, :, None] == jnp.arange(stores)[None, None, :]
    wanted = jnp.sum(jnp.where(at_store, (slots % held)[:, :, None], 0), axis=1).reshape(-1)

    def node(first, second):
        first, second = (first + SIDE) % SIDE, (second + SIDE) % SIDE
        return jnp.where(core == 0, second * SIDE + first, first * SIDE + second)

    first = jnp.where(core == 0, x, y)
    second = jnp.where(core == 0, y, x)
    picks = [
        node(first, second + target) * stores + node(first + arrival, second)
        for target in (1, 2, -1)
        for arrival in (0, -1, 1, 2)
    ]
    pick_at = jnp.stack(picks)
    entries = pick_at[:, None] == jnp.arange(requests * stores)[None, :]
    index = jnp.sum(jnp.where(entries, wanted[None, :], 0), axis=1).astype(jnp.int32)

    up, down = pick(index, own, before, behind, k_far, v_far)
    up, down = second_axis(up, 1), second_axis(down, -1)

    own_slots = jnp.sum(jnp.where((jnp.arange(requests) == req)[:, None], slots, 0), axis=0)
    store, local = own_slots // held, own_slots % held
    store_y, store_x = store // SIDE, store % SIDE
    one = order_of((jnp.where(core == 0, store_x, store_y) - first) % SIDE)
    two = order_of((jnp.where(core == 0, store_y, store_x) - second) % SIDE)
    array = jnp.where(two == 0, one, 3 + two)
    entry = jnp.where(two == 0, local, one)
    offset = jnp.where(two == 0, held, 4)
    shared = (array != 3) & (array != 6)
    where = jnp.stack([array, entry, jnp.where(shared, entry + offset, entry)]).astype(jnp.int32)

    positions = sel_index[0]
    sel = positions.shape[0]
    ctx = chosen_count * block
    everywhere = jnp.arange(ctx, dtype=jnp.int32)
    replaced = jnp.any(positions[:, None] == everywhere[None, :], axis=0)
    kpos = jnp.where(replaced, HIDDEN_POS, everywhere).reshape(chosen_count, block)
    qpos = jnp.broadcast_to(positions[:, None], (sel, 128))
    count = positions[ROWS - 1 :: ROWS] // block + 1
    q_cos, q_sin = tables(positions)
    angles = (*tables(everywhere[:block]), *tables(everywhere[::block]))

    place = jnp.stack(
        [((z + s + SIDE) % SIDE) * 2 + core for s in (0, -1, 1, 2)]
        + [((z + s + SIDE) % SIDE) * 2 + 1 - core for s in (0, -1, 1, 2)]
    ).astype(jnp.int32)
    pieces = [normed, z_before, z_behind, z_far, near, remote]
    low, new_k, new_v = project(place, pieces, 0, w_query, (w_key, w_value), q_cos, q_sin)
    up_first, down_first, _ = lax.optimization_barrier((up, down, low))
    k_last, v_last = second_axis(up_first[8:], 1), second_axis(down_first[8:], -1)
    (high,) = project(place, pieces, 1, w_query, (), q_cos, q_sin)
    mixed = attend(
        where, count, low, high, new_k, new_v, qpos, kpos, positions[None], angles,
        [own, before, behind, k_far, v_far, up, down, k_last, v_last],
    )
    return mixed[None]


def solution(mesh):
    placed = (
        P("req", "tp", None),
        P(),
        P(None, "tp"),
        P(None, "tp"),
        P(None, "tp"),
        P("req", None, "tp", None),
        P("req", None, "tp", None),
        P(),
        P(),
        P("req", None),
    )
    return jax.shard_map(
        on_device, mesh=mesh, in_specs=placed, out_specs=P("req", None, "tp"), check_vma=False
    )
```

```python
import functools

import jax
import jax.numpy as jnp
from jax import lax
from jax.experimental import pallas as pl
from jax.experimental.pallas import tpu as pltpu
from jax.sharding import PartitionSpec as P

BF16 = jnp.bfloat16
F32 = jnp.float32
SIDE = 4
ROWS = 128
STEP = 4
THETA = 500000.0
EPS = 1e-05
HIDDEN_POS = 1 << 30
MIB = 1 << 20


def move(value, step):
    pairs = []
    for y in range(SIDE):
        for x in range(SIDE):
            for z in range(SIDE):
                for core in range(2):
                    ty, tx, tz, tc = step(y, x, z, core)
                    source = ((y * SIDE + x) * SIDE + z) * 2 + core
                    target = (((ty % SIDE) * SIDE + tx % SIDE) * SIDE + tz % SIDE) * 2 + tc
                    pairs.append((source, target))
    return lax.ppermute(value, ("req", "tp"), pairs)


def first_axis(value, step):
    return move(value, lambda y, x, z, c: (y, x + step, z, c) if c == 0 else (y + step, x, z, c))


def second_axis(value, step):
    return move(value, lambda y, x, z, c: (y + step, x, z, c) if c == 0 else (y, x + step, z, c))


def along_z(value, step):
    return move(value, lambda y, x, z, c: (y, x, z + step, c))


def around_z(value):
    return move(value, lambda y, x, z, c: (y, x, z + 1 - 2 * c, c))


def other_core(value):
    return move(value, lambda y, x, z, c: (y, x, z, 1 - c))


def norm_kernel(tokens_ref, gain_ref, first_ref, out_ref):
    hidden = tokens_ref[...].astype(F32)
    scale = lax.rsqrt(jnp.mean(hidden * hidden, axis=-1, keepdims=True) + EPS)
    out_ref[...] = (hidden * scale * gain_ref[...].astype(F32)[None, :]).astype(BF16)


def normalise(tokens, gain, first):
    vmem = pl.BlockSpec(memory_space=pltpu.VMEM)
    return pl.pallas_call(
        norm_kernel,
        out_shape=jax.ShapeDtypeStruct(tokens.shape, BF16),
        in_specs=[vmem, vmem, pl.BlockSpec(memory_space=pl.ANY)],
        out_specs=vmem,
        compiler_params=pltpu.CompilerParams(vmem_limit_bytes=8 * MIB),
        name="norm",
    )(tokens, gain, first)


def pick_kernel(index_ref, own, before, behind, k_far, v_far, up, down):
    sources = (own, before, behind)
    held = k_far.shape[0]
    for slot in range(4):
        for target in range(3):
            n = index_ref[target * 4 + slot]
            keys = sources[slot].at[n] if slot < 3 else k_far.at[n]
            values = sources[slot].at[held + n] if slot < 3 else v_far.at[n]
            if target == 0:
                up[slot] = keys[...]
                up[4 + slot] = values[...]
            elif target == 1:
                up[8 + slot] = keys[...]
                down[8 + slot] = values[...]
            else:
                down[slot] = keys[...]
                down[4 + slot] = values[...]


def pick(index, own, before, behind, k_far, v_far):
    _, tokens, dim = own.shape
    vmem = pl.BlockSpec(memory_space=pltpu.VMEM)
    return pl.pallas_call(
        pick_kernel,
        out_shape=[jax.ShapeDtypeStruct((12, tokens, dim), BF16)] * 2,
        in_specs=[pl.BlockSpec(memory_space=pltpu.SMEM)] + [vmem] * 5,
        out_specs=[vmem] * 2,
        compiler_params=pltpu.CompilerParams(vmem_limit_bytes=10 * MIB),
        cost_estimate=pl.CostEstimate(flops=0, bytes_accessed=6 * MIB, transcendentals=0),
        name="pick",
    )(index, own, before, behind, k_far, v_far)


def rope(values, cosine, sine):
    return values * cosine + pltpu.roll(values, 64, 1) * sine


def project_kernel(with_kv, *refs):
    place_ref, p0, p1, p2, p3, near, remote = refs[:7]
    if with_kv:
        wq_ref, wk_hbm, wv_hbm, cos_ref, sin_ref, q_ref, nk_ref, nv_ref = refs[7:15]
        x_buf, x_sems, wk_buf, wv_buf, w_sems = refs[15:]
        k_copy = pltpu.make_async_copy(wk_hbm, wk_buf, w_sems.at[0])
        v_copy = pltpu.make_async_copy(wv_hbm, wv_buf, w_sems.at[1])
    else:
        wq_ref, cos_ref, sin_ref, q_ref, x_buf, x_sems = refs[7:]
    step = pl.program_id(0)
    rows = p0.shape[0]
    pieces = [p0, p1, p2, p3]
    pieces += [ref.at[pl.ds(n * rows, rows)] for ref in (near, remote) for n in range(ref.shape[0] // rows)]

    def piece_copy(n):
        at = pl.multiple_of(place_ref[n] * rows, 16)
        return pltpu.make_async_copy(pieces[n], x_buf.at[pl.ds(at, rows)], x_sems.at[n])

    @pl.when(step == 0)
    def _():
        for n in range(8):
            piece_copy(n).start()
        if with_kv:
            k_copy.start()
            v_copy.start()
        for n in range(8):
            piece_copy(n).wait()

    cosine = cos_ref[...]
    sine = sin_ref[...]

    @pl.when(step < 2)
    def _():
        raw = jnp.dot(x_buf[...], wq_ref[...], preferred_element_type=F32)
        for h in range(2):
            q_ref[h] = rope(raw[:, h * 128 : (h + 1) * 128], cosine, sine).astype(BF16)

    if with_kv:

        @pl.when(step == 2)
        def _():
            k_copy.wait()
            v_copy.wait()
            new_k = jnp.dot(x_buf[...], wk_buf[...], preferred_element_type=F32).astype(BF16)
            nk_ref[...] = rope(new_k.astype(F32), cosine, sine).astype(BF16)
            nv_ref[...] = jnp.dot(x_buf[...], wv_buf[...], preferred_element_type=F32).astype(BF16)


def project(place, pieces, half, w_query, w_kv, cosine, sine):
    rows, width = pieces[0].shape
    sel = 8 * rows
    any_spec = pl.BlockSpec(memory_space=pl.ANY)
    whole = pl.BlockSpec((sel, 128), lambda i: (0, 0))
    last = lambda i: jnp.minimum(i, 1)
    new = [jax.ShapeDtypeStruct((sel, 128), BF16)] * len(w_kv)
    scratch = [pltpu.VMEM((sel, width), BF16), pltpu.SemaphoreType.DMA((8,))]
    if w_kv:
        scratch += [pltpu.VMEM((width, 128), BF16)] * 2 + [pltpu.SemaphoreType.DMA((2,))]
    return pl.pallas_call(
        functools.partial(project_kernel, bool(w_kv)),
        grid=(3 if w_kv else 2,),
        out_shape=[jax.ShapeDtypeStruct((4, sel, 128), BF16)] + new,
        in_specs=[pl.BlockSpec(memory_space=pltpu.SMEM)]
        + [any_spec] * 6
        + [pl.BlockSpec((width, 256), lambda i: (0, 2 * half + last(i)))]
        + [any_spec] * len(w_kv)
        + [whole, whole],
        out_specs=[pl.BlockSpec((2, sel, 128), lambda i: (last(i), 0, 0))] + [whole] * len(w_kv),
        scratch_shapes=scratch,
        compiler_params=pltpu.CompilerParams(vmem_limit_bytes=40 * MIB),
        cost_estimate=pl.CostEstimate(
            flops=0, bytes_accessed=MIB, transcendentals=0
        ),
        name="project",
    )(place, *pieces, w_query, *w_kv, cosine, sine)


def attend_kernel(
    where_ref, count_ref, low_ref, high_ref, nk_ref, nv_ref, qpos_ref, kpos_ref, npos_ref, cos_ref, sin_ref, far_cos_ref, far_sin_ref, *refs
):
    own, before, behind, k_far, v_far, up, down, k_last, v_last, out_ref = refs[:10]
    k_buf, v_buf, nv_buf, q_buf, s_buf, m_buf, acc, sems = refs[10:]
    keys = (own, before, behind, k_far, up, down, k_last)
    values = (own, before, behind, v_far, up, down, v_last)
    block = k_buf.shape[1]
    blocks = k_buf.shape[0]
    heads, sel, dim = 2 * low_ref.shape[0], *low_ref.shape[1:]
    ctx = block * blocks
    tall = heads * ROWS
    factor = 1.4426950408889634 / (dim ** 0.5)

    def k_dest(j):
        return k_buf.at[j]

    def v_dest(j):
        return v_buf.at[pl.ds(j * block, block), pl.ds(0, dim)]

    for j in range(blocks):
        for n in range(7):

            @pl.when(where_ref[0, j] == n)
            def _():
                pltpu.make_async_copy(keys[n].at[where_ref[1, j]], k_dest(j), sems.at[0, j]).start()
                pltpu.make_async_copy(values[n].at[where_ref[2, j]], v_dest(j), sems.at[1, j]).start()

    v_buf[:, dim:] = jnp.ones((ctx, dim), BF16)
    nv_buf[:, dim:] = jnp.ones((sel, dim), BF16)
    nv_buf[:, :dim] = nv_ref[...]

    for j in range(blocks):
        pltpu.make_async_copy(keys[0].at[0], k_dest(j), sems.at[0, j]).wait()
        far_cos, far_sin = far_cos_ref[j : j + 1, :], far_sin_ref[j : j + 1, :]
        cosine = far_cos * cos_ref[...] - far_sin * sin_ref[...]
        sine = far_sin * cos_ref[...] + far_cos * sin_ref[...]
        k_buf[j] = rope(k_buf[j].astype(F32), cosine, sine).astype(BF16)
    for j in range(blocks):
        pltpu.make_async_copy(values[0].at[0], v_dest(j), sems.at[1, j]).wait()

    def masked_scores(queries, key_block, key_pos, query_pos):
        width = key_block.shape[0]
        scores = lax.dot_general(
            queries, key_block, (((1,), (1,)), ((), ())), preferred_element_type=F32
        )
        reps = width // 128
        seen = key_pos <= jnp.concatenate([query_pos] * reps, axis=1)
        scores = jnp.where(seen[None], scores.reshape(heads, ROWS, width), -jnp.inf)
        scores = scores.reshape(tall, width)
        most = scores[:, :128]
        for n in range(1, reps):
            most = jnp.maximum(most, scores[:, n * 128 : (n + 1) * 128])
        return scores, most

    def tile(i, carry):
        rows = pl.ds(pl.multiple_of(i * ROWS, ROWS), ROWS)
        half = tall // 2
        q_buf[:half] = low_ref[:, rows, :].reshape(half, dim)
        q_buf[half:] = high_ref[:, rows, :].reshape(half, dim)
        queries = q_buf[...]
        query_pos = qpos_ref[rows, :]
        scores, most = masked_scores(queries, nk_ref[...], npos_ref[...], query_pos)
        s_buf[:, ctx:] = scores
        m_buf[...] = most
        count = count_ref[i]

        def first(at, blocks_now):
            span = blocks_now * block
            scores, most = masked_scores(
                q_buf[...],
                k_buf[pl.ds(at, blocks_now)].reshape(span, dim),
                jnp.concatenate([kpos_ref[pl.ds(at + n, 1), :] for n in range(blocks_now)], axis=1),
                qpos_ref[rows, :],
            )
            s_buf[:, pl.ds(pl.multiple_of(at * block, block), span)] = scores
            m_buf[...] = jnp.maximum(m_buf[...], most)

        def over_blocks(body):
            def some(j, carry):
                body(j * STEP, STEP)
                return carry

            lax.fori_loop(0, count // STEP, some, 0)

            @pl.when(count % STEP >= 2)
            def _():
                body(count // STEP * STEP, 2)

            @pl.when(count % 2 == 1)
            def _():
                body(count - 1, 1)

        over_blocks(first)
        m_buf[...] = jnp.broadcast_to(jnp.max(m_buf[...], axis=1, keepdims=True), (tall, 128))

        def expos(scores):
            most = jnp.concatenate([m_buf[...]] * (scores.shape[1] // 128), axis=1)
            return jnp.exp2((scores - most) * factor).astype(BF16)

        acc[...] = jnp.dot(expos(s_buf[:, ctx:]), nv_buf[...], preferred_element_type=F32)

        def second(at, blocks_now):
            span = pl.ds(pl.multiple_of(at * block, block), blocks_now * block)
            acc[...] += jnp.dot(expos(s_buf[:, span]), v_buf[span, :], preferred_element_type=F32)

        over_blocks(second)
        result = (acc[:, :dim] / acc[:, dim:]).astype(BF16)
        for h in range(heads):
            out_ref[rows, h * dim : (h + 1) * dim] = result[h * ROWS : (h + 1) * ROWS]
        return carry

    lax.fori_loop(0, sel // ROWS, tile, 0)


def attend(where, count, low, high, new_k, new_v, qpos, kpos, npos, angles, arrays):
    heads, sel, dim = 2 * low.shape[0], *low.shape[1:]
    _, block, _ = arrays[0].shape
    blocks = kpos.shape[0]
    ctx = block * blocks
    smem = pl.BlockSpec(memory_space=pltpu.SMEM)
    vmem = pl.BlockSpec(memory_space=pltpu.VMEM)
    any_spec = pl.BlockSpec(memory_space=pl.ANY)
    tall = heads * ROWS
    return pl.pallas_call(
        attend_kernel,
        out_shape=jax.ShapeDtypeStruct((sel, heads * dim), BF16),
        in_specs=[smem] * 2 + [vmem] * 11 + [any_spec] * 9,
        out_specs=vmem,
        scratch_shapes=[
            pltpu.VMEM((blocks, block, dim), BF16),
            pltpu.VMEM((ctx, 2 * dim), BF16),
            pltpu.VMEM((sel, 2 * dim), BF16),
            pltpu.VMEM((tall, dim), BF16),
            pltpu.VMEM((tall, ctx + sel), F32),
            pltpu.VMEM((tall, 128), F32),
            pltpu.VMEM((tall, 2 * dim), F32),
            pltpu.SemaphoreType.DMA((2, blocks)),
        ],
        compiler_params=pltpu.CompilerParams(vmem_limit_bytes=40 * MIB),
        cost_estimate=pl.CostEstimate(
            flops=4 * heads * sel * ctx * dim, bytes_accessed=8 * MIB, transcendentals=heads * sel * ctx
        ),
        name="attend",
    )(where, count, low, high, new_k, new_v, qpos, kpos, npos, *angles, *arrays)


def tables(positions):
    frequency = THETA ** (-(2.0 / 128) * jnp.arange(64).astype(F32))
    angles = positions.astype(F32)[:, None] * frequency[None, :]
    cosine, sine = jnp.cos(angles), jnp.sin(angles)
    return jnp.concatenate([cosine, cosine], axis=1), jnp.concatenate([-sine, sine], axis=1)


def order_of(offset):
    return jnp.where(offset == 0, 0, jnp.where(offset == 2, 3, jnp.where(offset == 3, 1, 2)))


def on_device(
    tokens, norm_gain, w_query, w_key, w_value, store_keys, store_values, block_slot, retrieval, sel_index
):
    held, block, _, dim = store_keys.shape
    requests, chosen_count = retrieval.shape
    stores = block_slot.shape[0] // held
    req, tp = lax.axis_index("req"), lax.axis_index("tp")
    y, x = req // SIDE, req % SIDE
    z, core = tp // 2, tp % 2
    own = jnp.concatenate(
        [store_keys.reshape(held, block, dim), store_values.reshape(held, block, dim)]
    )
    before, behind = first_axis(own, 1), first_axis(own, -1)
    normed = normalise(tokens[0], norm_gain, own)
    z_before, z_behind = along_z(normed, 1), along_z(normed, -1)
    k_half, v_half = before[:held], behind[held:]
    k_far, v_far = first_axis(k_half, 1), first_axis(v_half, -1)
    z_before, z_behind, _, _ = lax.optimization_barrier((z_before, z_behind, k_half, v_half))
    z_far = around_z(jnp.where(core == 0, z_before, z_behind))
    near = other_core(jnp.concatenate([normed, z_before, z_behind]))
    remote = other_core(z_far)

    hot = retrieval[:, :, None] == jnp.arange(block_slot.shape[0])[None, None, :]
    slots = jnp.sum(jnp.where(hot, block_slot[None, None, :], 0), axis=2)
    at_store = (slots // held)[:, :, None] == jnp.arange(stores)[None, None, :]
    wanted = jnp.sum(jnp.where(at_store, (slots % held)[:, :, None], 0), axis=1).reshape(-1)

    def node(first, second):
        first, second = (first + SIDE) % SIDE, (second + SIDE) % SIDE
        return jnp.where(core == 0, second * SIDE + first, first * SIDE + second)

    first = jnp.where(core == 0, x, y)
    second = jnp.where(core == 0, y, x)
    picks = [
        node(first, second + target) * stores + node(first + arrival, second)
        for target in (1, 2, -1)
        for arrival in (0, -1, 1, 2)
    ]
    pick_at = jnp.stack(picks)
    entries = pick_at[:, None] == jnp.arange(requests * stores)[None, :]
    index = jnp.sum(jnp.where(entries, wanted[None, :], 0), axis=1).astype(jnp.int32)

    up, down = pick(index, own, before, behind, k_far, v_far)
    up, down = second_axis(up, 1), second_axis(down, -1)

    own_slots = jnp.sum(jnp.where((jnp.arange(requests) == req)[:, None], slots, 0), axis=0)
    store, local = own_slots // held, own_slots % held
    store_y, store_x = store // SIDE, store % SIDE
    one = order_of((jnp.where(core == 0, store_x, store_y) - first) % SIDE)
    two = order_of((jnp.where(core == 0, store_y, store_x) - second) % SIDE)
    array = jnp.where(two == 0, one, 3 + two)
    entry = jnp.where(two == 0, local, one)
    offset = jnp.where(two == 0, held, 4)
    shared = (array != 3) & (array != 6)
    where = jnp.stack([array, entry, jnp.where(shared, entry + offset, entry)]).astype(jnp.int32)

    positions = sel_index[0]
    sel = positions.shape[0]
    ctx = chosen_count * block
    everywhere = jnp.arange(ctx, dtype=jnp.int32)
    replaced = jnp.any(positions[:, None] == everywhere[None, :], axis=0)
    kpos = jnp.where(replaced, HIDDEN_POS, everywhere).reshape(chosen_count, block)
    qpos = jnp.broadcast_to(positions[:, None], (sel, 128))
    count = positions[ROWS - 1 :: ROWS] // block + 1
    q_cos, q_sin = tables(positions)
    angles = (*tables(everywhere[:block]), *tables(everywhere[::block]))

    place = jnp.stack(
        [((z + s + SIDE) % SIDE) * 2 + core for s in (0, -1, 1, 2)]
        + [((z + s + SIDE) % SIDE) * 2 + 1 - core for s in (0, -1, 1, 2)]
    ).astype(jnp.int32)
    pieces = [normed, z_before, z_behind, z_far, near, remote]
    low, new_k, new_v = project(place, pieces, 0, w_query, (w_key, w_value), q_cos, q_sin)
    up_first, down_first, _ = lax.optimization_barrier((up, down, low))
    k_last, v_last = second_axis(up_first[8:], 1), second_axis(down_first[8:], -1)
    (high,) = project(place, pieces, 1, w_query, (), q_cos, q_sin)
    mixed = attend(
        where, count, low, high, new_k, new_v, qpos, kpos, positions[None], angles,
        [own, before, behind, k_far, v_far, up, down, k_last, v_last],
    )
    return mixed[None]


def solution(mesh):
    placed = (
        P("req", "tp", None),
        P(),
        P(None, "tp"),
        P(None, "tp"),
        P(None, "tp"),
        P("req", None, "tp", None),
        P("req", None, "tp", None),
        P(),
        P(),
        P("req", None),
    )
    return jax.shard_map(
        on_device, mesh=mesh, in_specs=placed, out_specs=P("req", None, "tp"), check_vma=False
    )
```
